512 devices in a mesh: seq: 16 (over x, z_hi), head: 32 (over y, z_lo, core).
Axes of the slice: x: 4, y: 8, z: 8 (z_hi: 4, z_lo: 2; z = z_hi * 2 + z_lo), core: 2. Of those that a mesh axis runs over, the one named last changes fastest.
Arguments:
- queries: bfloat16 [4096, 4096], P('seq', 'head'), may hold values from -8 to 8
- block_keys: bfloat16 [4096, 512], P('seq'), may hold values from -8 to 8
- block_values: bfloat16 [4096, 512], P('seq'), may hold values from -12 to 12
- cache_keys: bfloat16 [4, 16384, 128], P(None, 'seq'), may hold values from -6 to 6
- cache_values: bfloat16 [4, 16384, 128], P(None, 'seq'), may hold values from -12 to 12
- lengths: int32 [8], replicated, may hold values from 1 to 4096, 16384 in all
- row_request: int32 [4096], P('seq'), may hold values from 0 to 7, never falling along the last dimension, each value on 1 to 4089 neighbouring positions
- positions: int32 [4096], P('seq'), may hold values from 0 to 1023
- out_weight: bfloat16 [4096, 4096], P('head'), may hold values from -0.375 to 0.375
Outputs:
- attended: bfloat16 [4096, 4096], P('seq', 'head')
The draws below stay inside these ranges and needn't reach their ends.
Inputs may be any that keep to these rules, and one draw needn't show every extreme that they name: `row_request`: rows of one request stand together, requests in increasing order; one request has 4089 rows and every other request exactly one. Every request has at least one committed token; the lengths sum to 16384.
All inputs are finite; a program needn't handle non-finite values.
Results may differ from the reference program's by a relative error of at most 0.014.
Values may be sent and summed in bfloat16 or wider, within the bound.
A program may use at most 64 MiB of HBM per device.

```python
import math
import jax
import jax.numpy as jnp
import numpy as np
from jax import lax

D = 4096
HEADS = 32
KVH = 4
HD = 128
REQS = 8
SPAN = 1024
ROWS = 4096
CTX = 16384


def draw_queries(key, part):
    key = jax.random.fold_in(key, 3)
    base = jax.random.truncated_normal(key, -4.0, 4.0, (ROWS, HEADS, HD), jnp.float32)
    return base.reshape(ROWS, HEADS * HD).astype(jnp.bfloat16)


def draw_block_keys(key, part):
    key = jax.random.fold_in(key, 7)
    base = jax.random.truncated_normal(key, -4.0, 4.0, (ROWS, KVH, HD), jnp.float32)
    return base.reshape(ROWS, KVH * HD).astype(jnp.bfloat16)


def plant(result, stream_key, least, high):
    place = [jax.random.randint(jax.random.fold_in(stream_key, axis), (), 0, length) for axis, length in enumerate(result.shape)]
    longest = result.shape.index(max(result.shape))
    neighbour = place[:longest] + [(place[longest] + 1) % result.shape[longest]] + place[longest + 1:]
    return result.at[tuple(place)].set(least).at[tuple(neighbour)].set(high)


def raised(values, own_key, source, target, blocks, factor):
    def block_of(position):
        return (jnp.arange(values.shape[position]) // (values.shape[position] // blocks)).reshape((-1,) + (1,) * (values.ndim - 1 - position))

    first = jax.random.permutation(own_key, blocks)[block_of(target)]
    second = (block_of(target) + blocks // 2) % blocks
    return jnp.where((block_of(source) == first) | (block_of(source) == second), factor * values, values)


def shard_levels(key, shape, split, least, top_value):
    level = 1.0
    for axis_at, shards_of in split:
        steps = jax.random.uniform(jax.random.fold_in(jax.random.fold_in(key, 6), axis_at), (shards_of,), jnp.float32, least / len(split), top_value / len(split))
        level = level * jnp.repeat(jnp.exp(steps), shape[axis_at] // shards_of).reshape((-1,) + (1,) * (len(shape) - 1 - axis_at))
    return level


def profile(amount, total, limit, slope):
    portions = [(1 << 20) // math.isqrt(grade ** slope) + 1 for grade in range(2, amount + 1)]
    surplus, counts = total - limit - (amount - 1), [1] * (amount - 1)
    while surplus > 0:
        movable = [i for i in range(amount - 1) if counts[i] < limit]
        whole, left = sum([portions[i] for i in movable]), surplus
        for i in movable:
            more = min(limit - counts[i], max(1, left * portions[i] // whole), surplus)
            counts[i] = counts[i] + more
            surplus = surplus - more
    return np.array([limit] + counts)


def uneven_parts(rng, amount, total, bound, skew):
    if amount == 2:
        one = jax.random.randint(rng, (), max(1, total - bound), min(bound, total - 1) + 1)
        return jnp.stack([one, total - one])
    sizes = jnp.asarray(profile(amount, total, bound, skew), jnp.int32)
    couples = (amount - 1) // 2
    donor, sink = sizes[1:1 + 2 * couples:2], sizes[2:2 + 2 * couples:2]
    margin = jnp.minimum(donor - 1, bound - sink)
    shifted = jax.random.randint(jax.random.fold_in(rng, 1), (couples,), 0, 1 << 20) % (margin + 1)
    sizes = sizes.at[1:1 + 2 * couples:2].set(donor - shifted).at[2:2 + 2 * couples:2].set(sink + shifted)
    return sizes[jax.random.permutation(jax.random.fold_in(rng, 2), amount)]


def normal_values(own_key, extent, spread, bound, shards=(), held_as=jnp.bfloat16):
    gain = shard_levels(own_key, extent, shards, -0.22, 0.18) if shards else 1.0
    values = jax.random.normal(own_key, extent, jnp.float32) * spread * gain
    return jnp.minimum(jnp.maximum(values, -bound), bound).astype(held_as)


def gaussian_with(own_key, shape, deviation, limit, split, heavy, kind=jnp.bfloat16):
    entries = deviation * jax.random.normal(own_key, shape, jnp.float32)
    if split:
        entries = entries * shard_levels(own_key, shape, split, -0.22, 0.18)
    return jnp.clip(raised(entries, jax.random.fold_in(own_key, 3), *heavy), -limit, limit).astype(kind)


def setup_inputs(seed: int = 0) -> dict:
    seeds = jax.random.split(jax.random.key(seed), 10)
    queries = draw_queries(jax.random.fold_in(seeds[9], 71), 0)
    block_keys = draw_block_keys(jax.random.fold_in(seeds[9], 71), 0)
    block_values = normal_values(seeds[2], (ROWS, KVH * HD), 2.0, 12.0, ((0, 16),))
    cache_keys = normal_values(seeds[3], (KVH, CTX, HD), 1.0, 6.0, ((1, 16),))
    cache_values = normal_values(seeds[4], (KVH, CTX, HD), 2.0, 12.0, ((1, 16),))
    lengths = uneven_parts(seeds[5], REQS, CTX, CTX // 4, 2).astype(jnp.int32)
    row_request = jnp.searchsorted(jnp.cumsum(uneven_parts(seeds[6], REQS, ROWS, ROWS - REQS + 1, 2)), jnp.arange(ROWS), side="right").astype(jnp.int32)
    positions = plant(jax.random.randint(seeds[7], (ROWS,), 0, SPAN), jax.random.fold_in(seeds[7], 1), 0, SPAN - 1).astype(jnp.int32)
    out_weight = gaussian_with(seeds[8], (HEADS * HD, D), (HEADS * HD // 4) ** -0.5, 0.375, ((0, 32),), (0, 1, 32, 2.75))
    return dict(queries=queries, block_keys=block_keys, block_values=block_values, cache_keys=cache_keys, cache_values=cache_values, lengths=lengths, row_request=row_request, positions=positions, out_weight=out_weight)


rope_base = 10000.0

def rotate_half_dims(vectors, rotary_pos):
    half_dim = vectors.shape[-1] // 2
    quarter = half_dim // 2
    freqs = jnp.exp(-math.log(rope_base) * jnp.arange(quarter, dtype=jnp.float32) / quarter)
    angles = rotary_pos[:, None] * freqs[None, :]
    cosine = jnp.cos(angles)[:, None, :]
    sine = jnp.sin(angles)[:, None, :]
    first = vectors[..., :quarter]
    second = vectors[..., quarter:half_dim]
    return jnp.concatenate([first * cosine - second * sine, second * cosine + first * sine, vectors[..., half_dim:]], axis=-1)

def reference(queries, block_keys, block_values, cache_keys, cache_values, lengths, row_request, positions, out_weight):
    starts = jnp.cumsum(lengths) - lengths
    row_len = lengths[row_request]
    row_lower = starts[row_request]
    row_upper = row_lower + row_len
    rotary_pos = (row_len + positions).astype(jnp.float32)
    q_rot = rotate_half_dims(queries.reshape(ROWS, HEADS, HD).astype(jnp.float32), rotary_pos).astype(jnp.bfloat16)
    k_rot = rotate_half_dims(block_keys.reshape(ROWS, KVH, HD).astype(jnp.float32), rotary_pos).astype(jnp.bfloat16)
    value_rows = block_values.reshape(ROWS, KVH, HD)
    all_keys = jnp.concatenate([cache_keys, jnp.transpose(k_rot, (1, 0, 2))], axis=1).astype(jnp.float32)
    all_values = jnp.concatenate([cache_values, jnp.transpose(value_rows, (1, 0, 2))], axis=1).astype(jnp.float32)
    key_tags = jnp.concatenate([jnp.arange(CTX, dtype=jnp.int32), -(row_request.astype(jnp.int32) + 1)])
    group_size = HEADS // KVH
    row_block = math.gcd(ROWS, 64)
    blocks = ROWS // row_block
    score_scale = 1.0 / math.sqrt(HD)

    def one_block(inputs):
        q_block, lower, upper, request = inputs
        grouped = q_block.reshape(row_block, KVH, group_size, HD).astype(jnp.float32)
        scores = jnp.einsum('rkgd,knd->rkgn', grouped, all_keys) * score_scale
        visible = (key_tags[None, :] >= lower[:, None]) & (key_tags[None, :] < upper[:, None]) | (key_tags[None, :] == -(request[:, None] + 1))
        visible = visible[:, None, None, :]
        masked = jnp.where(visible, scores, -jnp.inf)
        largest = lax.optimization_barrier(jnp.max(masked, axis=-1, keepdims=True))
        weights = jnp.where(visible, jnp.exp(scores - largest), 0.0)
        totals = lax.optimization_barrier(jnp.sum(weights, axis=-1))
        rounded = weights.astype(jnp.bfloat16).astype(jnp.float32)
        summed = jnp.einsum('rkgn,knd->rkgd', rounded, all_values)
        return (summed / totals[..., None]).reshape(row_block, HEADS * HD).astype(jnp.bfloat16)
    heads_out = lax.map(one_block, (q_rot.reshape(blocks, row_block, HEADS, HD), row_lower.reshape(blocks, row_block), row_upper.reshape(blocks, row_block), row_request.reshape(blocks, row_block)))
    heads_out = heads_out.reshape(ROWS, HEADS * HD)
    return jnp.dot(heads_out, out_weight, preferred_element_type=jnp.float32).astype(jnp.bfloat16)
```

```python
import math

import jax
import jax.numpy as jnp
from jax import lax
from jax.experimental import pallas as pl
from jax.experimental.pallas import tpu as pltpu
from jax.sharding import PartitionSpec as P

HD = 128
REQS = 8
BIG = 4089
MASKED = -1e30
SCALE = math.log2(math.e) / math.sqrt(HD)
LN2 = math.log(2.0)

bf16 = jnp.bfloat16
f32 = jnp.float32
i32 = jnp.int32
MESH = pl.DeviceIdType.MESH


def kernel(
    len_s, req_s, req_v, pos_v, q_h, bk_h, bv_h, ck_h, cv_h, w_h,
    out_ref,
    qraw, kraw, cosb, sinb, qbuf, qhot, cand, gkv, bias, cks, cvs, qs, sp, spr,
    ob, tb, lb, osend, ssend, orecv, srecv, hbuf, wbuf, psend, precv,
    loc, sq, rq, sc, rc, sz, rz, sg, rg, ss, rs, sw, rw, so, ro, sl, rl, sh, rh, sf, rf,
):
    seq = lax.axis_index("seq")
    head = lax.axis_index("head")
    x, zh = seq // 4, seq % 4
    g, m = head // 8, head % 8
    chip, core = m // 2, m % 2

    def xpeer(k):
        return (((x + k) % 4) * 4 + zh, head)

    def zpeer(k):
        return (x * 4 + (zh + k) % 4, head)

    def gpeer(k, other):
        c = (1 - core) if other else core
        return (seq, g * 8 + ((chip + k) % 4) * 2 + c)

    def fpeer(k):
        return (seq, ((g + k) % 4) * 8 + m)

    def remote(src, dst, ssem, rsem, peer):
        return pltpu.make_async_remote_copy(
            src_ref=src, dst_ref=dst, send_sem=ssem, recv_sem=rsem,
            device_id=peer, device_id_type=MESH,
        )

    piece = pl.multiple_of(32 * m, 32)
    gcol = pl.multiple_of(g * 128, 128)
    mycand = pl.multiple_of(256 * x + 32 * m, 32)
    c_q = pltpu.make_async_copy(q_h, qraw, loc.at[0])
    c_k = pltpu.make_async_copy(bk_h.at[pl.ds(piece, 32), pl.ds(gcol, 128)], kraw, loc.at[1])
    c_v = pltpu.make_async_copy(
        bv_h.at[pl.ds(piece, 32), pl.ds(gcol, 128)], gkv.at[0, 1, 0, 0, 0], loc.at[2]
    )
    c_ck = pltpu.make_async_copy(ck_h.at[g, pl.ds(mycand, 32)], cand.at[0, 0], loc.at[3])
    c_cv = pltpu.make_async_copy(cv_h.at[g, pl.ds(mycand, 32)], cand.at[1, 0], loc.at[4])
    c_sk = pltpu.make_async_copy(ck_h.at[g], cks, loc.at[5])
    c_sv = pltpu.make_async_copy(cv_h.at[g], cvs, loc.at[6])
    for c in (c_q, c_k, c_v, c_ck, c_cv, c_sk, c_sv):
        c.start()

    barrier = pltpu.get_barrier_semaphore()
    peers = [xpeer(k) for k in (1, 2, 3)] + [zpeer(k) for k in (1, 2, 3)]
    peers += [gpeer(k, o) for k in range(4) for o in (False, True) if k or o]
    peers += [fpeer(k) for k in (1, 3)]
    for peer in peers:
        pl.semaphore_signal(barrier, inc=1, device_id=peer, device_id_type=MESH)

    row_len = jnp.zeros((2, 128), i32)
    for r in range(REQS):
        row_len = jnp.where(req_v[...] == r, len_s[r], row_len)
    rotary = (row_len + pos_v[...]).astype(f32)
    spread = jnp.concatenate(
        [jnp.transpose(jnp.broadcast_to(rotary[h : h + 1, :], (128, 128))) for h in (0, 1)], axis=0
    )
    lane8 = lax.broadcasted_iota(i32, (8, 128), 1)
    freqs = jnp.zeros((8, 128), f32)
    for k in range(HD // 4):
        freqs = jnp.where((lane8 < 64) & (lane8 % 32 == k), 10000.0 ** (-k / (HD // 4)), freqs)
    angles = spread * freqs[0:1, :]
    lane256 = lax.broadcasted_iota(i32, (256, 128), 1)
    cosb[...] = jnp.cos(angles)
    sine = jnp.sin(angles)
    sinb[...] = jnp.where(lane256 < 32, -sine, sine)

    def rotate(v, cosine, signed, lane):
        partner = jnp.where(lane < 32, pltpu.roll(v, 96, 1), pltpu.roll(v, 32, 1))
        return v * cosine + partner * signed

    pl.semaphore_wait(barrier, len(peers))

    order = (2, 1, 3)
    cand_c, q_c, blk_c = [], [], []
    for k in order:
        start = pl.multiple_of(256 * ((x + k) % 4) + 32 * m, 32)
        cand_c.append(remote(ck_h.at[g, pl.ds(start, 32)], cand.at[0, k], sc.at[0, k], rc.at[0, k], xpeer(k)))
        cand_c.append(remote(cv_h.at[g, pl.ds(start, 32)], cand.at[1, k], sc.at[1, k], rc.at[1, k], xpeer(k)))
        blk_c.append(
            remote(gkv.at[0, :, 0, 0, 0], gkv.at[0, :, 0, 0, k], sz.at[0, k], rz.at[0, k], zpeer(k))
        )
        q_c.append(remote(qbuf.at[0], qbuf.at[k], sq.at[k], rq.at[k], xpeer(k)))
    for c in cand_c:
        c.start()

    c_k.wait()
    gkv[0, 0, 0, 0, 0] = rotate(
        kraw[...].astype(f32), cosb[pl.ds(piece, 32), :], sinb[pl.ds(piece, 32), :],
        lax.broadcasted_iota(i32, (32, 128), 1),
    ).astype(bf16)
    c_v.wait()
    for c in blk_c:
        c.start()
    c_q.wait()
    qbuf[0] = rotate(qraw[...].astype(f32), cosb[...], sinb[...], lane256).astype(bf16)
    for c in q_c:
        c.start()

    def blocks_start(kc, ko):
        mm = ((chip + kc) % 4) * 2 + ((1 - core) if ko else core)
        for j in range(4):
            col = pl.multiple_of((((g + j) % 4) * 8 + mm) * 128, 128)
            src = w_h.at[:, pl.ds(col, 128)]
            dst = wbuf.at[kc, ko, :, j * 128 : (j + 1) * 128]
            if kc == 0 and ko == 0:
                pltpu.make_async_copy(src, dst, loc.at[7]).start()
            else:
                remote(src, dst, sw.at[kc, ko], rw.at[kc, ko], gpeer(kc, ko == 1)).start()

    blocks_start(0, 0)
    blocks_start(0, 1)

    big = req_s[128]
    first = jnp.int32(0)
    span = jnp.int32(0)
    run = jnp.int32(0)
    low8 = jnp.zeros((8, 128), i32)
    high8 = jnp.zeros((8, 128), i32)
    for r in range(REQS):
        size = len_s[r]
        hit = big == r
        first = jnp.where(hit, run, first)
        span = jnp.where(hit, size, span)
        low8 = jnp.where(lane8 == r, run, low8)
        run = run + size
        high8 = jnp.where(lane8 == r, run, high8)
    high8 = jnp.where(lane8 == big, low8, high8)

    def request_of(row):
        return jnp.where(row < big, row, jnp.where(row < big + BIG, big, row - (BIG - 1)))

    for c in cand_c:
        c.wait_recv()
    c_ck.wait()
    c_cv.wait()
    row32 = lax.broadcasted_iota(i32, (32, 128), 0)
    for t in (0, 1):
        chosen = jnp.zeros((32, 128), f32)
        for k in range(4):
            token = 4096 * ((x + 4 - k) % 4) + 1024 * zh + 256 * x + 32 * m + row32
            ok = (token >= first) & (token < first + span)
            chosen = jnp.where(ok, cand[t, k].astype(f32), chosen)
        gkv[1, t, 0, 0, 0] = chosen.astype(bf16)
    zc_c = [
        remote(gkv.at[1, :, 0, 0, 0], gkv.at[1, :, 0, 0, k], sz.at[1, k], rz.at[1, k], zpeer(k))
        for k in order
    ]
    for c in zc_c:
        c.start()

    def spread_start(kind):
        cs = [
            remote(gkv.at[kind, :, 0, 0], gkv.at[kind, :, k, 0], sg.at[kind, k, 0], rg.at[kind, k, 0], gpeer(k, False))
            for k in (1, 2, 3)
        ]
        cs.append(
            remote(gkv.at[kind, :, 0, 0], gkv.at[kind, :, 0, 1], sg.at[kind, 0, 1], rg.at[kind, 0, 1], gpeer(0, True))
        )
        for c in cs:
            c.start()
        return cs

    def relay(kind, cs):
        fs = []
        for k in (1, 2, 3):
            cs[k - 1].wait_recv()
            f = remote(
                gkv.at[kind, :, k, 0], gkv.at[kind, :, k, 1], sg.at[kind, k, 1], rg.at[kind, k, 1], gpeer(0, True)
            )
            f.start()
            fs.append(f)
        return fs

    def relay_wait(cs, fs):
        cs[3].wait_recv()
        for f in fs:
            f.wait_recv()

    for c in blk_c:
        c.wait_recv()
    blk_g = spread_start(0)

    for c in q_c:
        c.wait_recv()
    at0, at3 = x, (x + 1) % 4
    qs[0, 0:16, :] = qbuf[at0, 0:16, :]
    qs[0, 16:32, :] = qbuf[at3, 240:256, :]
    qs_c = [remote(qs.at[0], qs.at[k], ss.at[0, k], rs.at[0, k], zpeer(k)) for k in order]
    for c in qs_c:
        c.start()

    for c in zc_c:
        c.wait_recv()
    cache_g = spread_start(1)

    key = lax.broadcasted_iota(i32, (1024, 128), 0)
    lane1024 = lax.broadcasted_iota(i32, (1024, 128), 1)
    key_chip = (chip + 4 - (key >> 8)) & 3
    key_core = (core + (key >> 7)) & 1
    key_z = (zh + 4 - (key >> 5)) & 3
    inner = 32 * (key_chip * 2 + key_core) + (key & 31)
    block_req = request_of(1024 * x + 256 * key_z + inner)
    bias[0] = jnp.where(lane1024 == block_req, 0.0, MASKED).astype(bf16)
    slot = 1024 * key_z + 256 * x + inner
    inside = ((slot - first) & 4095) < span
    bias[1] = jnp.where(inside & (lane1024 == big), 0.0, MASKED).astype(bf16)
    row256 = lax.broadcasted_iota(i32, (256, 128), 0)
    for k in range(4):
        row = 256 * (4 * ((x + 4 - k) % 4) + zh) + row256
        qhot[k] = jnp.where(lane256 == request_of(row), 1.0, 0.0).astype(bf16)

    def attend(kind, k, v_t):
        k_aug = jnp.concatenate([gkv[kind, 0].reshape(1024, 128), bias[kind]], axis=1)
        q_aug = jnp.concatenate([qbuf[k], qhot[k]], axis=1)
        s = lax.dot_general(k_aug, q_aug, (((1,), (1,)), ((), ())), preferred_element_type=f32)
        top = jnp.max(s, axis=0, keepdims=True) * SCALE
        p = jnp.exp2(s * SCALE - top)
        total = jnp.sum(p, axis=0, keepdims=True)
        o = jnp.dot(v_t, p.astype(bf16), preferred_element_type=f32)
        return o, top, total

    def merge(o1, t1, l1, o2, t2, l2):
        top = jnp.maximum(t1, t2)
        w1, w2 = jnp.exp2(t1 - top), jnp.exp2(t2 - top)
        return o1 * w1 + o2 * w2, top, l1 * w1 + l2 * w2

    for c in qs_c:
        c.wait_recv()
    c_sk.wait()
    c_sv.wait()
    row128 = lax.broadcasted_iota(i32, (128, 128), 0)
    lane128 = lax.broadcasted_iota(i32, (128, 128), 1)
    from_z = (zh + 4 - (row128 >> 5)) & 3
    late = (row128 >> 4) & 1
    qs_row = 256 * from_z + (row128 & 15) + late * (3072 + 240)
    qs_hot = jnp.where(lane128 == request_of(qs_row), 1.0, 0.0).astype(bf16)
    token = 1024 * seq + key
    seen = (token >= low8[0:1, :]) & (token < high8[0:1, :])
    own_bias = jnp.where(seen, 0.0, MASKED).astype(bf16)
    s = lax.dot_general(
        jnp.concatenate([qs[...].reshape(128, 128), qs_hot], axis=1),
        jnp.concatenate([cks[...], own_bias], axis=1),
        (((1,), (1,)), ((), ())), preferred_element_type=f32,
    )
    top = jnp.max(s, axis=1, keepdims=True) * SCALE
    p = jnp.exp2(s * SCALE - top)
    total = jnp.sum(p, axis=1, keepdims=True)
    o = jnp.dot(p.astype(bf16), cvs[...], preferred_element_type=f32) / total
    lse = jnp.broadcast_to(top + jnp.log(total) * (1.0 / LN2), (128, 128))
    sp[:, 0] = o.reshape(4, 32, 128)
    sp[:, 1] = lse.reshape(4, 32, 128)
    sp_c = [
        remote(sp.at[k], spr.at[k], ss.at[1, k], rs.at[1, k], (x * 4 + (zh + 4 - k) % 4, head)) for k in order
    ]
    for c in sp_c:
        c.start()

    blk_f = relay(0, blk_g)
    relay_wait(blk_g, blk_f)

    vt0 = jnp.transpose(gkv[0, 1].reshape(1024, 128))

    def block_step(k, carry):
        o, t, l = attend(0, k, vt0)
        ob[k] = o
        tb[k] = jnp.broadcast_to(t, (8, 256))
        lb[k] = jnp.broadcast_to(l, (8, 256))
        return carry

    lax.fori_loop(0, 4, block_step, 0)

    cache_f = relay(1, cache_g)
    for kc in (2, 1, 3):
        blocks_start(kc, 0)
        blocks_start(kc, 1)

    for c in sp_c:
        c.wait_recv()
    o, t, l = sp[0, 0], sp[0, 1], jnp.ones((32, 128), f32)
    for k in (1, 2, 3):
        o, t, l = merge(o, t, l, spr[k, 0], spr[k, 1], 1.0)
    pad = jnp.zeros((96, 128), f32)
    o, t, l = [jnp.transpose(jnp.concatenate([a, pad], axis=0)) for a in (o, t, l)]
    for at, half, shift, own in ((at0, 0, 0, lane128 < 16), (at3, 1, 96, lane128 >= 112)):
        cols = slice(128 * half, 128 * half + 128)
        o2, t2, l2 = [pltpu.roll(a, shift, 1) if shift else a for a in (o, t, l)]
        t2 = jnp.where(own, t2, MASKED)[0:8, :]
        l2 = l2[0:8, :]
        t1, l1 = tb[at, :, cols], lb[at, :, cols]
        top = jnp.maximum(t1, t2)
        w1, w2 = jnp.exp2(t1 - top), jnp.exp2(t2 - top)
        tb[at, :, cols] = top
        lb[at, :, cols] = l1 * w1 + l2 * w2
        ob[at, :, cols] = ob[at, :, cols] * w1[0:1, :] + jnp.where(own, o2, 0.0) * w2[0:1, :]

    relay_wait(cache_g, cache_f)
    vt1 = jnp.transpose(gkv[1, 1].reshape(1024, 128))
    o_c = []
    for k in order + (0,):
        o, t, l = attend(1, k, vt1)
        o, t, l = merge(ob[k], tb[k, 0:1, :], lb[k, 0:1, :], o, t, l)
        osend[k] = (o * (1.0 / l)).astype(bf16)
        ssend[k] = jnp.broadcast_to(t + jnp.log(l) * (1.0 / LN2), (8, 256))
        if k:
            back = (((x + 4 - k) % 4) * 4 + zh, head)
            o_c.append(remote(osend.at[k], orecv.at[k], so.at[k], ro.at[k], back))
            o_c.append(remote(ssend.at[k], srecv.at[k], sl.at[k], rl.at[k], back))
            o_c[-2].start()
            o_c[-1].start()
    for c in o_c:
        c.wait_recv()

    lses = [ssend[0, 0:1, :]] + [srecv[k, 0:1, :] for k in (1, 2, 3)]
    top = jnp.maximum(jnp.maximum(lses[0], lses[1]), jnp.maximum(lses[2], lses[3]))
    weights = [jnp.exp2(l - top) for l in lses]
    total = 1.0 / (weights[0] + weights[1] + weights[2] + weights[3])
    h_c = []
    for half in (0, 1):
        cols = slice(128 * half, 128 * half + 128)
        heads = osend[0, :, cols].astype(f32) * (weights[0] * total)[:, cols]
        for k in (1, 2, 3):
            heads = heads + orecv[k, :, cols].astype(f32) * (weights[k] * total)[:, cols]
        hbuf[half, 0, 0] = jnp.transpose(heads).astype(bf16)
        cs = [
            remote(
                hbuf.at[half, 0, 0], hbuf.at[half, k, 0], sh.at[half, k, 0], rh.at[half, k, 0], gpeer(k, False)
            )
            for k in order
        ]
        cs.append(
            remote(hbuf.at[half, 0, 0], hbuf.at[half, 0, 1], sh.at[half, 0, 1], rh.at[half, 0, 1], gpeer(0, True))
        )
        for c in cs:
            c.start()
        h_c.append(cs)
    h_f = []
    for half in (0, 1):
        fs = []
        for n, k in enumerate(order):
            h_c[half][n].wait_recv()
            f = remote(
                hbuf.at[half, k, 0], hbuf.at[half, k, 1], sh.at[half, k, 1], rh.at[half, k, 1], gpeer(0, True)
            )
            f.start()
            fs.append(f)
        h_f.append(fs)

    w_wait = []
    for kc in range(4):
        for ko in (0, 1):
            if kc or ko:
                w_wait.append(
                    remote(w_h.at[:, 0:512], wbuf.at[kc, ko], sw.at[kc, ko], rw.at[kc, ko], gpeer(kc, ko == 1))
                )
    for c in w_wait:
        c.wait_recv()
    pltpu.make_async_copy(w_h.at[:, 0:512], wbuf.at[0, 0], loc.at[7]).wait()

    own, mids, finals = [], [], []
    for half in (0, 1):
        h_c[half][3].wait_recv()
        for f in h_f[half]:
            f.wait_recv()
        lhs = jnp.concatenate([hbuf[half, kc, ko] for kc in range(4) for ko in (0, 1)], axis=1)
        acc = jnp.dot(lhs, wbuf[...].reshape(1024, 512), preferred_element_type=f32)
        fwd, bwd = (1, 3) if half == 0 else (3, 1)
        psend[half, 2] = acc[:, 256:384].astype(bf16)
        psend[half, bwd] = acc[:, bwd * 128 : bwd * 128 + 128].astype(bf16)
        mid = remote(psend.at[half, 2], precv.at[half, 2], sf.at[half, 2], rf.at[half, 2], fpeer(fwd))
        near = remote(psend.at[half, bwd], precv.at[half, bwd], sf.at[half, bwd], rf.at[half, bwd], fpeer(bwd))
        mid.start()
        near.start()
        mids.append(mid)
        finals.append(near)
        own.append((acc[:, 0:128], acc[:, fwd * 128 : fwd * 128 + 128]))
    for half in (0, 1):
        fwd = 1 if half == 0 else 3
        mids[half].wait_recv()
        psend[half, fwd] = (own[half][1] + precv[half, 2].astype(f32)).astype(bf16)
        far = remote(psend.at[half, fwd], precv.at[half, fwd], sf.at[half, fwd], rf.at[half, fwd], fpeer(fwd))
        far.start()
        finals.append(far)
    for half in (0, 1):
        finals[half].wait_recv()
        finals[2 + half].wait_recv()
        total = own[half][0] + precv[half, 1].astype(f32) + precv[half, 3].astype(f32)
        out_ref[128 * half : 128 * half + 128, :] = total.astype(bf16)

    sent = cand_c + q_c + blk_c + zc_c + blk_g + blk_f + cache_g + cache_f + qs_c + sp_c
    sent += w_wait + o_c + h_c[0] + h_c[1] + h_f[0] + h_f[1] + mids + finals
    for c in sent:
        c.wait_send()


def shards(queries, block_keys, block_values, cache_keys, cache_values, lengths, row_request, positions, out_weight):
    dma = pltpu.SemaphoreType.DMA
    vmem = pltpu.VMEM
    return pl.pallas_call(
        kernel,
        out_shape=jax.ShapeDtypeStruct((256, HD), bf16),
        in_specs=[pl.BlockSpec(memory_space=pltpu.SMEM)] * 2
        + [pl.BlockSpec(memory_space=pltpu.VMEM)] * 2
        + [pl.BlockSpec(memory_space=pl.ANY)] * 6,
        out_specs=pl.BlockSpec(memory_space=pltpu.VMEM),
        scratch_shapes=[
            vmem((256, 128), bf16),
            vmem((32, 128), bf16),
            vmem((256, 128), f32),
            vmem((256, 128), f32),
            vmem((4, 256, 128), bf16),
            vmem((4, 256, 128), bf16),
            vmem((2, 4, 32, 128), bf16),
            vmem((2, 2, 4, 2, 4, 32, 128), bf16),
            vmem((2, 1024, 128), bf16),
            vmem((1024, 128), bf16),
            vmem((1024, 128), bf16),
            vmem((4, 32, 128), bf16),
            vmem((4, 2, 32, 128), f32),
            vmem((4, 2, 32, 128), f32),
            vmem((4, 128, 256), f32),
            vmem((4, 8, 256), f32),
            vmem((4, 8, 256), f32),
            vmem((4, 128, 256), bf16),
            vmem((4, 8, 256), f32),
            vmem((4, 128, 256), bf16),
            vmem((4, 8, 256), f32),
            vmem((2, 4, 2, 128, 128), bf16),
            vmem((4, 2, 128, 512), bf16),
            vmem((2, 4, 128, 128), bf16),
            vmem((2, 4, 128, 128), bf16),
            dma((8,)),
            dma((4,)), dma((4,)),
            dma((2, 4)), dma((2, 4)),
            dma((2, 4)), dma((2, 4)),
            dma((2, 4, 2)), dma((2, 4, 2)),
            dma((2, 4)), dma((2, 4)),
            dma((4, 2)), dma((4, 2)),
            dma((4,)), dma((4,)),
            dma((4,)), dma((4,)),
            dma((2, 4, 2)), dma((2, 4, 2)),
            dma((2, 4)), dma((2, 4)),
        ],
        compiler_params=pltpu.CompilerParams(
            collective_id=0, has_side_effects=True, vmem_limit_bytes=63 * 1024 * 1024
        ),
    )(
        lengths, row_request, row_request.reshape(2, 128), positions.reshape(2, 128),
        queries, block_keys, block_values, cache_keys, cache_values, out_weight,
    )


def solution(mesh):
    placed = (
        P("seq", "head"),
        P("seq", None),
        P("seq", None),
        P(None, "seq", None),
        P(None, "seq", None),
        P(),
        P("seq"),
        P("seq"),
        P("head", None),
    )
    return jax.shard_map(
        shards, mesh=mesh, in_specs=placed, out_specs=P("seq", "head"), check_vma=False
    )
```

```python
import math

import jax
import jax.numpy as jnp
from jax import lax
from jax.experimental import pallas as pl
from jax.experimental.pallas import tpu as pltpu
from jax.sharding import PartitionSpec as P

HD = 128
REQS = 8
BIG = 4089
MASKED = -1e30
SCALE = math.log2(math.e) / math.sqrt(HD)
LN2 = math.log(2.0)

bf16 = jnp.bfloat16
f32 = jnp.float32
i32 = jnp.int32
MESH = pl.DeviceIdType.MESH


def kernel(
    len_h, req_h, rows_h, pos_h, q_h, bk_h, bv_h, ck_h, cv_h, w_h,
    out_ref,
    len_s, req_s, req_v, pos_v, qraw, kraw, cosb, sinb, qbuf, qhot, cand, gkv, bias, cks, cvs, qs, sp, spr,
    ob, tb, lb, osend, ssend, orecv, srecv, hbuf, wbuf, psend, precv,
    loc, sq, rq, sc, rc, sz, rz, sg, rg, ss, rs, sw, rw, so, ro, sl, rl, sh, rh, sf, rf,
):
    seq = lax.axis_index("seq")
    head = lax.axis_index("head")
    x, zh = seq // 4, seq % 4
    g, m = head // 8, head % 8
    chip, core = m // 2, m % 2

    def xpeer(k):
        return (((x + k) % 4) * 4 + zh, head)

    def zpeer(k):
        return (x * 4 + (zh + k) % 4, head)

    def gpeer(k, other):
        c = (1 - core) if other else core
        return (seq, g * 8 + ((chip + k) % 4) * 2 + c)

    def fpeer(k):
        return (seq, ((g + k) % 4) * 8 + m)

    def remote(src, dst, ssem, rsem, peer):
        return pltpu.make_async_remote_copy(
            src_ref=src, dst_ref=dst, send_sem=ssem, recv_sem=rsem,
            device_id=peer, device_id_type=MESH,
        )

    piece = pl.multiple_of(32 * m, 32)
    gcol = pl.multiple_of(g * 128, 128)
    mycand = pl.multiple_of(256 * x + 32 * m, 32)
    c_q = pltpu.make_async_copy(q_h, qraw, loc.at[0])
    c_k = pltpu.make_async_copy(bk_h.at[pl.ds(piece, 32), pl.ds(gcol, 128)], kraw, loc.at[1])
    c_v = pltpu.make_async_copy(
        bv_h.at[pl.ds(piece, 32), pl.ds(gcol, 128)], gkv.at[0, 1, 0, 0, 0], loc.at[2]
    )
    c_ck = pltpu.make_async_copy(ck_h.at[g, pl.ds(mycand, 32)], cand.at[0, 0], loc.at[3])
    c_cv = pltpu.make_async_copy(cv_h.at[g, pl.ds(mycand, 32)], cand.at[1, 0], loc.at[4])
    c_sk = pltpu.make_async_copy(ck_h.at[g], cks, loc.at[5])
    c_sv = pltpu.make_async_copy(cv_h.at[g], cvs, loc.at[6])
    c_small = [
        pltpu.make_async_copy(src, dst, loc.at[8 + n])
        for n, (src, dst) in enumerate(((rows_h, req_v), (pos_h, pos_v), (len_h, len_s), (req_h, req_s)))
    ]
    for c in c_small + [c_k, c_v, c_q, c_ck, c_cv, c_sk, c_sv]:
        c.start()

    barrier = pltpu.get_barrier_semaphore()
    peers = [xpeer(k) for k in (1, 2, 3)] + [zpeer(k) for k in (1, 2, 3)]
    peers += [gpeer(k, o) for k in range(4) for o in (False, True) if k or o]
    peers += [fpeer(k) for k in (1, 3)]
    for peer in peers:
        pl.semaphore_signal(barrier, inc=1, device_id=peer, device_id_type=MESH)

    pl.semaphore_wait(barrier, len(peers))

    order = (2, 1, 3)
    cand_c, q_c, blk_c = [], [], []
    for k in order:
        start = pl.multiple_of(256 * ((x + k) % 4) + 32 * m, 32)
        cand_c.append(remote(ck_h.at[g, pl.ds(start, 32)], cand.at[0, k], sc.at[0, k], rc.at[0, k], xpeer(k)))
        cand_c.append(remote(cv_h.at[g, pl.ds(start, 32)], cand.at[1, k], sc.at[1, k], rc.at[1, k], xpeer(k)))
        blk_c.append(
            remote(gkv.at[0, :, 0, 0, 0], gkv.at[0, :, 0, 0, k], sz.at[0, k], rz.at[0, k], zpeer(k))
        )
        q_c.append(remote(qbuf.at[0], qbuf.at[k], sq.at[k], rq.at[k], xpeer(k)))
    for c in cand_c:
        c.start()

    for c in c_small:
        c.wait()
    row_len = jnp.zeros((2, 128), i32)
    for r in range(REQS):
        row_len = jnp.where(req_v[...] == r, len_s[r], row_len)
    rotary = (row_len + pos_v[...]).astype(f32)
    spread = jnp.concatenate(
        [jnp.transpose(jnp.broadcast_to(rotary[h : h + 1, :], (128, 128))) for h in (0, 1)], axis=0
    )
    lane8 = lax.broadcasted_iota(i32, (8, 128), 1)
    turns = jnp.zeros((8, 128), f32)
    for k in range(HD // 4):
        turns = jnp.where(
            (lane8 < 64) & (lane8 % 32 == k), 10000.0 ** (-k / (HD // 4)) / (2.0 * math.pi), turns
        )
    lane256 = lax.broadcasted_iota(i32, (256, 128), 1)
    angle = spread * turns[0:1, :]
    angle = (angle - jnp.floor(angle + 0.5)) * (2.0 * math.pi)
    square = angle * angle
    cosine = jnp.full((256, 128), 1.0 / math.factorial(16), f32)
    sine = jnp.full((256, 128), -1.0 / math.factorial(15), f32)
    for n in range(7, -1, -1):
        cosine = cosine * square + (-1.0) ** n / math.factorial(2 * n)
    for n in range(6, -1, -1):
        sine = sine * square + (-1.0) ** n / math.factorial(2 * n + 1)
    sine = sine * angle
    cosb[...] = cosine
    sinb[...] = jnp.where(lane256 < 32, -sine, sine)

    def rotate(v, cosine, signed, lane):
        partner = jnp.where(lane < 32, pltpu.roll(v, 96, 1), pltpu.roll(v, 32, 1))
        return v * cosine + partner * signed

    def spread_piece(kind, z):
        src = gkv.at[kind, :, 0, 0, z]
        for k in (3, 1, 2):
            remote(src, gkv.at[kind, :, k, 0, z], sg.at[kind, k, 0], rg.at[kind, k, 0], gpeer(k, False)).start()
        remote(src, gkv.at[kind, :, 0, 1, z], sg.at[kind, 0, 1], rg.at[kind, 0, 1], gpeer(0, True)).start()

    def spread_all(kind):
        cs = [
            remote(gkv.at[kind, :, 0, 0], gkv.at[kind, :, k, 0], sg.at[kind, k, 0], rg.at[kind, k, 0], gpeer(k, False))
            for k in (1, 2, 3)
        ]
        cs.append(
            remote(gkv.at[kind, :, 0, 0], gkv.at[kind, :, 0, 1], sg.at[kind, 0, 1], rg.at[kind, 0, 1], gpeer(0, True))
        )
        return cs

    c_k.wait()
    gkv[0, 0, 0, 0, 0] = rotate(
        kraw[...].astype(f32), cosb[pl.ds(piece, 32), :], sinb[pl.ds(piece, 32), :],
        lax.broadcasted_iota(i32, (32, 128), 1),
    ).astype(bf16)
    c_v.wait()
    for c in blk_c:
        c.start()
    spread_piece(0, 0)
    c_q.wait()
    qbuf[0] = rotate(qraw[...].astype(f32), cosb[...], sinb[...], lane256).astype(bf16)
    for c in q_c:
        c.start()

    def blocks_start(kc, ko):
        mm = ((chip + kc) % 4) * 2 + ((1 - core) if ko else core)
        for j in range(4):
            col = pl.multiple_of((((g + j) % 4) * 8 + mm) * 128, 128)
            src = w_h.at[:, pl.ds(col, 128)]
            dst = wbuf.at[kc, ko, :, j * 128 : (j + 1) * 128]
            if kc == 0 and ko == 0:
                pltpu.make_async_copy(src, dst, loc.at[7]).start()
            else:
                remote(src, dst, sw.at[kc, ko], rw.at[kc, ko], gpeer(kc, ko == 1)).start()

    big = req_s[128]
    first = jnp.int32(0)
    span = jnp.int32(0)
    run = jnp.int32(0)
    low8 = jnp.zeros((8, 128), i32)
    high8 = jnp.zeros((8, 128), i32)
    for r in range(REQS):
        size = len_s[r]
        hit = big == r
        first = jnp.where(hit, run, first)
        span = jnp.where(hit, size, span)
        low8 = jnp.where(lane8 == r, run, low8)
        run = run + size
        high8 = jnp.where(lane8 == r, run, high8)
    high8 = jnp.where(lane8 == big, low8, high8)

    def request_of(row):
        return jnp.where(row < big, row, jnp.where(row < big + BIG, big, row - (BIG - 1)))

    key = lax.broadcasted_iota(i32, (1024, 128), 0)
    lane1024 = lax.broadcasted_iota(i32, (1024, 128), 1)
    key_chip = (chip + 4 - (key >> 8)) & 3
    key_core = (core + (key >> 7)) & 1
    key_z = (zh + 4 - (key >> 5)) & 3
    inner = 32 * (key_chip * 2 + key_core) + (key & 31)
    block_req = request_of(1024 * x + 256 * key_z + inner)
    bias[0] = jnp.where(lane1024 == block_req, 0.0, MASKED).astype(bf16)
    slot = 1024 * key_z + 256 * x + inner
    inside = ((slot - first) & 4095) < span
    bias[1] = jnp.where(inside & (lane1024 == big), 0.0, MASKED).astype(bf16)
    row256 = lax.broadcasted_iota(i32, (256, 128), 0)
    for k in range(4):
        row = 256 * (4 * ((x + 4 - k) % 4) + zh) + row256
        qhot[k] = jnp.where(lane256 == request_of(row), 1.0, 0.0).astype(bf16)

    for c in cand_c:
        c.wait_recv()
    c_ck.wait()
    c_cv.wait()
    row32 = lax.broadcasted_iota(i32, (32, 128), 0)
    for t in (0, 1):
        chosen = jnp.zeros((32, 128), f32)
        for k in range(4):
            token = 4096 * ((x + 4 - k) % 4) + 1024 * zh + 256 * x + 32 * m + row32
            ok = (token >= first) & (token < first + span)
            chosen = jnp.where(ok, cand[t, k].astype(f32), chosen)
        gkv[1, t, 0, 0, 0] = chosen.astype(bf16)
    zc_c = [
        remote(gkv.at[1, :, 0, 0, 0], gkv.at[1, :, 0, 0, k], sz.at[1, k], rz.at[1, k], zpeer(k))
        for k in order
    ]
    for c in zc_c:
        c.start()
    spread_piece(1, 0)

    blk_c[1].wait_recv()
    spread_piece(0, 1)
    blk_c[2].wait_recv()
    spread_piece(0, 3)

    for c in q_c:
        c.wait_recv()
    at0, at3 = x, (x + 1) % 4
    qs[0, 0:16, :] = qbuf[at0, 0:16, :]
    qs[0, 16:32, :] = qbuf[at3, 240:256, :]
    qs_c = [remote(qs.at[0], qs.at[k], ss.at[0, k], rs.at[0, k], zpeer(k)) for k in order]
    for c in qs_c:
        c.start()

    row128 = lax.broadcasted_iota(i32, (128, 128), 0)
    lane128 = lax.broadcasted_iota(i32, (128, 128), 1)
    from_z = (zh + 4 - (row128 >> 5)) & 3
    late = (row128 >> 4) & 1
    qs_row = 256 * from_z + (row128 & 15) + late * (3072 + 240)
    qs_hot = jnp.where(lane128 == request_of(qs_row), 1.0, 0.0).astype(bf16)
    token = 1024 * seq + key
    seen = (token >= low8[0:1, :]) & (token < high8[0:1, :])
    bias[2] = jnp.where(seen, 0.0, MASKED).astype(bf16)
    zc_c[1].wait_recv()
    spread_piece(1, 1)
    zc_c[2].wait_recv()
    spread_piece(1, 3)
    blk_c[0].wait_recv()
    spread_piece(0, 2)
    zc_c[0].wait_recv()
    spread_piece(1, 2)
    blk_g, cache_g = spread_all(0), spread_all(1)
    blocks_start(0, 0)
    blocks_start(0, 1)
    blocks_start(1, 0)

    def relay(kind, cs):
        fs = []
        for k in (1, 2, 3):
            cs[k - 1].wait_recv()
            f = remote(
                gkv.at[kind, :, k, 0], gkv.at[kind, :, k, 1], sg.at[kind, k, 1], rg.at[kind, k, 1], gpeer(0, True)
            )
            f.start()
            fs.append(f)
        return fs

    def relay_wait(cs, fs):
        cs[3].wait_recv()
        for f in fs:
            f.wait_recv()

    def attend(kind, k, v_t):
        k_aug = jnp.concatenate([gkv[kind, 0].reshape(1024, 128), bias[kind]], axis=1)
        q_aug = jnp.concatenate([qbuf[k], qhot[k]], axis=1)
        s = lax.dot_general(k_aug, q_aug, (((1,), (1,)), ((), ())), preferred_element_type=f32)
        top = jnp.max(s, axis=0, keepdims=True) * SCALE
        p = jnp.exp2(s * SCALE - top)
        total = jnp.sum(p, axis=0, keepdims=True)
        o = jnp.dot(v_t, p.astype(bf16), preferred_element_type=f32)
        return o, top, total

    def merge(o1, t1, l1, o2, t2, l2):
        top = jnp.maximum(t1, t2)
        w1, w2 = jnp.exp2(t1 - top), jnp.exp2(t2 - top)
        return o1 * w1 + o2 * w2, top, l1 * w1 + l2 * w2

    for c in qs_c:
        c.wait_recv()
    c_sk.wait()
    c_sv.wait()
    s = lax.dot_general(
        jnp.concatenate([qs[...].reshape(128, 128), qs_hot], axis=1),
        jnp.concatenate([cks[...], bias[2]], axis=1),
        (((1,), (1,)), ((), ())), preferred_element_type=f32,
    )
    top = jnp.max(s, axis=1, keepdims=True) * SCALE
    p = jnp.exp2(s * SCALE - top)
    total = jnp.sum(p, axis=1, keepdims=True)
    o = jnp.dot(p.astype(bf16), cvs[...], preferred_element_type=f32) / total
    lse = jnp.broadcast_to(top + jnp.log(total) * (1.0 / LN2), (128, 128))
    sp[:, 0] = o.reshape(4, 32, 128)
    sp[:, 1] = lse.reshape(4, 32, 128)
    sp_c = [
        remote(sp.at[k], spr.at[k], ss.at[1, k], rs.at[1, k], (x * 4 + (zh + 4 - k) % 4, head)) for k in order
    ]
    for c in sp_c:
        c.start()

    blk_f = relay(0, blk_g)
    relay_wait(blk_g, blk_f)

    vt0 = jnp.transpose(gkv[0, 1].reshape(1024, 128))

    def block_step(k, carry):
        o, t, l = attend(0, k, vt0)
        ob[k] = o
        tb[k] = jnp.broadcast_to(t, (8, 256))
        lb[k] = jnp.broadcast_to(l, (8, 256))
        return carry

    lax.fori_loop(0, 4, block_step, 0)

    cache_f = relay(1, cache_g)
    for kc, ko in ((3, 0), (3, 1), (1, 1), (2, 0), (2, 1)):
        blocks_start(kc, ko)

    for c in sp_c:
        c.wait_recv()
    o, t, l = sp[0, 0], sp[0, 1], jnp.ones((32, 128), f32)
    for k in (1, 2, 3):
        o, t, l = merge(o, t, l, spr[k, 0], spr[k, 1], 1.0)
    pad = jnp.zeros((96, 128), f32)
    o, t, l = [jnp.transpose(jnp.concatenate([a, pad], axis=0)) for a in (o, t, l)]
    for at, half, shift, own in ((at0, 0, 0, lane128 < 16), (at3, 1, 96, lane128 >= 112)):
        cols = slice(128 * half, 128 * half + 128)
        o2, t2, l2 = [pltpu.roll(a, shift, 1) if shift else a for a in (o, t, l)]
        t2 = jnp.where(own, t2, MASKED)[0:8, :]
        l2 = l2[0:8, :]
        t1, l1 = tb[at, :, cols], lb[at, :, cols]
        top = jnp.maximum(t1, t2)
        w1, w2 = jnp.exp2(t1 - top), jnp.exp2(t2 - top)
        tb[at, :, cols] = top
        lb[at, :, cols] = l1 * w1 + l2 * w2
        ob[at, :, cols] = ob[at, :, cols] * w1[0:1, :] + jnp.where(own, o2, 0.0) * w2[0:1, :]

    relay_wait(cache_g, cache_f)
    vt1 = jnp.transpose(gkv[1, 1].reshape(1024, 128))
    o_c = []
    for k in order + (0,):
        o, t, l = attend(1, k, vt1)
        o, t, l = merge(ob[k], tb[k, 0:1, :], lb[k, 0:1, :], o, t, l)
        osend[k] = (o * (1.0 / l)).astype(bf16)
        ssend[k] = jnp.broadcast_to(t + jnp.log(l) * (1.0 / LN2), (8, 256))
        if k:
            back = (((x + 4 - k) % 4) * 4 + zh, head)
            o_c.append(remote(osend.at[k], orecv.at[k], so.at[k], ro.at[k], back))
            o_c.append(remote(ssend.at[k], srecv.at[k], sl.at[k], rl.at[k], back))
            o_c[-2].start()
            o_c[-1].start()
    for c in cand_c + q_c + blk_c + zc_c + blk_g + blk_f + cache_g + cache_f + qs_c + sp_c:
        c.wait_send()
    for c in o_c:
        c.wait_recv()

    lses = [ssend[0, 0:1, :]] + [srecv[k, 0:1, :] for k in (1, 2, 3)]
    top = jnp.maximum(jnp.maximum(lses[0], lses[1]), jnp.maximum(lses[2], lses[3]))
    weights = [jnp.exp2(l - top) for l in lses]
    total = 1.0 / (weights[0] + weights[1] + weights[2] + weights[3])
    h_c = []
    for half in (0, 1):
        cols = slice(128 * half, 128 * half + 128)
        heads = osend[0, :, cols].astype(f32) * (weights[0] * total)[:, cols]
        for k in (1, 2, 3):
            heads = heads + orecv[k, :, cols].astype(f32) * (weights[k] * total)[:, cols]
        hbuf[half, 0, 0] = jnp.transpose(heads).astype(bf16)
        cs = [
            remote(
                hbuf.at[half, 0, 0], hbuf.at[half, k, 0], sh.at[half, k, 0], rh.at[half, k, 0], gpeer(k, False)
            )
            for k in order
        ]
        cs.append(
            remote(hbuf.at[half, 0, 0], hbuf.at[half, 0, 1], sh.at[half, 0, 1], rh.at[half, 0, 1], gpeer(0, True))
        )
        for c in cs:
            c.start()
        h_c.append(cs)
    h_f = []
    for half in (0, 1):
        fs = []
        for n, k in enumerate(order):
            h_c[half][n].wait_recv()
            f = remote(
                hbuf.at[half, k, 0], hbuf.at[half, k, 1], sh.at[half, k, 1], rh.at[half, k, 1], gpeer(0, True)
            )
            f.start()
            fs.append(f)
        h_f.append(fs)

    w_wait = []
    for kc in range(4):
        for ko in (0, 1):
            if kc or ko:
                w_wait.append(
                    remote(w_h.at[:, 0:512], wbuf.at[kc, ko], sw.at[kc, ko], rw.at[kc, ko], gpeer(kc, ko == 1))
                )
    for c in w_wait:
        c.wait_recv()
    pltpu.make_async_copy(w_h.at[:, 0:512], wbuf.at[0, 0], loc.at[7]).wait()

    own, mids, finals = [], [], []
    for half in (0, 1):
        h_c[half][3].wait_recv()
        for f in h_f[half]:
            f.wait_recv()
        lhs = jnp.concatenate([hbuf[half, kc, ko] for kc in range(4) for ko in (0, 1)], axis=1)
        acc = jnp.dot(lhs, wbuf[...].reshape(1024, 512), preferred_element_type=f32)
        fwd, bwd = (1, 3) if half == 0 else (3, 1)
        psend[half, 2] = acc[:, 256:384].astype(bf16)
        psend[half, bwd] = acc[:, bwd * 128 : bwd * 128 + 128].astype(bf16)
        mid = remote(psend.at[half, 2], precv.at[half, 2], sf.at[half, 2], rf.at[half, 2], fpeer(fwd))
        near = remote(psend.at[half, bwd], precv.at[half, bwd], sf.at[half, bwd], rf.at[half, bwd], fpeer(bwd))
        mid.start()
        near.start()
        mids.append(mid)
        finals.append(near)
        own.append((acc[:, 0:128], acc[:, fwd * 128 : fwd * 128 + 128]))
    for c in o_c + h_c[0] + h_c[1] + h_f[0] + h_f[1]:
        c.wait_send()
    for half in (0, 1):
        fwd = 1 if half == 0 else 3
        mids[half].wait_recv()
        psend[half, fwd] = (own[half][1] + precv[half, 2].astype(f32)).astype(bf16)
        far = remote(psend.at[half, fwd], precv.at[half, fwd], sf.at[half, fwd], rf.at[half, fwd], fpeer(fwd))
        far.start()
        finals.append(far)
    for c in w_wait:
        c.wait_send()
    for half in (0, 1):
        finals[half].wait_recv()
        finals[2 + half].wait_recv()
        total = own[half][0] + precv[half, 1].astype(f32) + precv[half, 3].astype(f32)
        out_ref[128 * half : 128 * half + 128, :] = total.astype(bf16)

    sent = mids + finals
    for c in sent:
        c.wait_send()


def shards(queries, block_keys, block_values, cache_keys, cache_values, lengths, row_request, positions, out_weight):
    dma = pltpu.SemaphoreType.DMA
    vmem = pltpu.VMEM
    return pl.pallas_call(
        kernel,
        out_shape=jax.ShapeDtypeStruct((256, HD), bf16),
        in_specs=[pl.BlockSpec(memory_space=pl.ANY)] * 10,
        out_specs=pl.BlockSpec(memory_space=pltpu.VMEM),
        scratch_shapes=[
            pltpu.SMEM((8,), i32),
            pltpu.SMEM((256,), i32),
            vmem((2, 128), i32),
            vmem((2, 128), i32),
            vmem((256, 128), bf16),
            vmem((32, 128), bf16),
            vmem((256, 128), f32),
            vmem((256, 128), f32),
            vmem((4, 256, 128), bf16),
            vmem((4, 256, 128), bf16),
            vmem((2, 4, 32, 128), bf16),
            vmem((2, 2, 4, 2, 4, 32, 128), bf16),
            vmem((3, 1024, 128), bf16),
            vmem((1024, 128), bf16),
            vmem((1024, 128), bf16),
            vmem((4, 32, 128), bf16),
            vmem((4, 2, 32, 128), f32),
            vmem((4, 2, 32, 128), f32),
            vmem((4, 128, 256), f32),
            vmem((4, 8, 256), f32),
            vmem((4, 8, 256), f32),
            vmem((4, 128, 256), bf16),
            vmem((4, 8, 256), f32),
            vmem((4, 128, 256), bf16),
            vmem((4, 8, 256), f32),
            vmem((2, 4, 2, 128, 128), bf16),
            vmem((4, 2, 128, 512), bf16),
            vmem((2, 4, 128, 128), bf16),
            vmem((2, 4, 128, 128), bf16),
            dma((12,)),
            dma((4,)), dma((4,)),
            dma((2, 4)), dma((2, 4)),
            dma((2, 4)), dma((2, 4)),
            dma((2, 4, 2)), dma((2, 4, 2)),
            dma((2, 4)), dma((2, 4)),
            dma((4, 2)), dma((4, 2)),
            dma((4,)), dma((4,)),
            dma((4,)), dma((4,)),
            dma((2, 4, 2)), dma((2, 4, 2)),
            dma((2, 4)), dma((2, 4)),
        ],
        compiler_params=pltpu.CompilerParams(
            collective_id=0, has_side_effects=True, vmem_limit_bytes=63 * 1024 * 1024
        ),
    )(
        lengths, row_request, row_request.reshape(2, 128), positions.reshape(2, 128),
        queries, block_keys, block_values, cache_keys, cache_values, out_weight,
    )


def solution(mesh):
    placed = (
        P("seq", "head"),
        P("seq", None),
        P("seq", None),
        P(None, "seq", None),
        P(None, "seq", None),
        P(),
        P("seq"),
        P("seq"),
        P("head", None),
    )
    return jax.shard_map(
        shards, mesh=mesh, in_specs=placed, out_specs=P("seq", "head"), check_vma=False
    )
```

```python
import math

import jax
import jax.numpy as jnp
from jax import lax
from jax.experimental import pallas as pl
from jax.experimental.pallas import tpu as pltpu
from jax.sharding import PartitionSpec as P

HD = 128
REQS = 8
BIG = 4089
MASKED = -1e30
SCALE = 1.0 / math.sqrt(HD)

bf16 = jnp.bfloat16
f32 = jnp.float32
i32 = jnp.int32
MESH = pl.DeviceIdType.MESH


def kernel(
    len_h, req_h, rows_h, pos_h, q_h, bk_h, bv_h, ck_h, cv_h, w_h,
    mine_ref, near_ref,
    len_s, req_s, req_v, pos_v, qraw, kraw, cosb, sinb, qbuf, qhot, cand, gkv, bias, cks, cvs, qx, qs, sp, spr,
    ob, tb, lb, osend, ssend, orecv, srecv, hbuf, wfull, wst, wbuf, psend, precv, own, wts,
    loc, sq, rq, sc, rc, sz, rz, sg, rg, ss, rs, sw, rw, sx, rx, so, ro, sl, rl, sh, rh, sf, rf,
):
    seq = lax.axis_index("seq")
    head = lax.axis_index("head")
    x, zh = seq // 4, seq % 4
    g, m = head // 8, head % 8
    chip, core = m // 2, m % 2

    def xpeer(k):
        return (((x + k) % 4) * 4 + zh, head)

    def zpeer(k):
        return (x * 4 + (zh + k) % 4, head)

    def gpeer(k, other):
        c = (1 - core) if other else core
        return (seq, g * 8 + ((chip + k) % 4) * 2 + c)

    def fpeer(k):
        return (seq, ((g + k) % 4) * 8 + m)

    def remote(src, dst, ssem, rsem, peer):
        return pltpu.make_async_remote_copy(
            src_ref=src, dst_ref=dst, send_sem=ssem, recv_sem=rsem,
            device_id=peer, device_id_type=MESH,
        )

    piece = pl.multiple_of(32 * m, 32)
    gcol = pl.multiple_of(g * 128, 128)
    mycand = pl.multiple_of(256 * x + 32 * m, 32)
    c_q = pltpu.make_async_copy(q_h, qraw, loc.at[0])
    c_k = pltpu.make_async_copy(bk_h.at[pl.ds(piece, 32), pl.ds(gcol, 128)], kraw, loc.at[1])
    c_v = pltpu.make_async_copy(
        bv_h.at[pl.ds(piece, 32), pl.ds(gcol, 128)], gkv.at[0, 1, 0, 0, 0], loc.at[2]
    )
    c_ck = pltpu.make_async_copy(ck_h.at[g, pl.ds(mycand, 32)], cand.at[0, 0], loc.at[3])
    c_cv = pltpu.make_async_copy(cv_h.at[g, pl.ds(mycand, 32)], cand.at[1, 0], loc.at[4])
    c_sk = pltpu.make_async_copy(ck_h.at[g], cks, loc.at[5])
    c_sv = pltpu.make_async_copy(cv_h.at[g], cvs, loc.at[6])
    c_small = [
        pltpu.make_async_copy(src, dst, loc.at[8 + n])
        for n, (src, dst) in enumerate(((rows_h, req_v), (pos_h, pos_v), (len_h, len_s), (req_h, req_s)))
    ]
    c_w = pltpu.make_async_copy(w_h, wfull, loc.at[7])
    for c in c_small + [c_k, c_v, c_q, c_ck, c_cv, c_sk, c_sv, c_w]:
        c.start()

    barrier = pltpu.get_barrier_semaphore()
    peers = [xpeer(k) for k in (1, 2, 3)] + [zpeer(k) for k in (1, 2, 3)]
    peers += [gpeer(k, o) for k in range(4) for o in (False, True) if k or o]
    peers += [fpeer(k) for k in (1, 3)]
    for peer in peers:
        pl.semaphore_signal(barrier, inc=1, device_id=peer, device_id_type=MESH)

    pl.semaphore_wait(barrier, len(peers))

    order = (2, 1, 3)
    cand_c, q_c, blk_c = [], [], []
    for k in order:
        start = pl.multiple_of(256 * ((x + k) % 4) + 32 * m, 32)
        cand_c.append(remote(ck_h.at[g, pl.ds(start, 32)], cand.at[0, k], sc.at[0, k], rc.at[0, k], xpeer(k)))
        cand_c.append(remote(cv_h.at[g, pl.ds(start, 32)], cand.at[1, k], sc.at[1, k], rc.at[1, k], xpeer(k)))
        blk_c.append(
            remote(gkv.at[0, :, 0, 0, 0], gkv.at[0, :, 0, 0, k], sz.at[0, k], rz.at[0, k], zpeer(k))
        )
        q_c.append(remote(qbuf.at[0], qbuf.at[k], sq.at[k], rq.at[k], xpeer(k)))
    for c in cand_c:
        c.start()

    for c in c_small:
        c.wait()
    row_len = jnp.zeros((2, 128), i32)
    for r in range(REQS):
        row_len = jnp.where(req_v[...] == r, len_s[r], row_len)
    rotary = (row_len + pos_v[...]).astype(f32)
    spread = jnp.concatenate(
        [jnp.transpose(jnp.broadcast_to(rotary[h : h + 1, :], (128, 128))) for h in (0, 1)], axis=0
    )
    lane8 = lax.broadcasted_iota(i32, (8, 128), 1)
    turns = jnp.zeros((8, 128), f32)
    for k in range(HD // 4):
        turns = jnp.where(
            (lane8 < 64) & (lane8 % 32 == k), 10000.0 ** (-k / (HD // 4)) / (2.0 * math.pi), turns
        )
    lane256 = lax.broadcasted_iota(i32, (256, 128), 1)
    angle = spread * turns[0:1, :]
    angle = (angle - jnp.floor(angle + 0.5)) * (2.0 * math.pi)
    square = angle * angle
    cosine = jnp.full((256, 128), 1.0 / math.factorial(16), f32)
    sine = jnp.full((256, 128), -1.0 / math.factorial(15), f32)
    for n in range(7, -1, -1):
        cosine = cosine * square + (-1.0) ** n / math.factorial(2 * n)
    for n in range(6, -1, -1):
        sine = sine * square + (-1.0) ** n / math.factorial(2 * n + 1)
    sine = sine * angle
    cosb[...] = cosine
    sinb[...] = jnp.where(lane256 < 32, -sine, sine)

    def rotate(v, cosine, signed, lane):
        partner = jnp.where(lane < 32, pltpu.roll(v, 96, 1), pltpu.roll(v, 32, 1))
        return v * cosine + partner * signed

    def spread_piece(kind, z):
        src = gkv.at[kind, :, 0, 0, z]
        for k in (3, 1, 2):
            remote(src, gkv.at[kind, :, k, 0, z], sg.at[kind, k, 0], rg.at[kind, k, 0], gpeer(k, False)).start()
        remote(src, gkv.at[kind, :, 0, 1, z], sg.at[kind, 0, 1], rg.at[kind, 0, 1], gpeer(0, True)).start()

    def spread_all(kind):
        cs = [
            remote(gkv.at[kind, :, 0, 0], gkv.at[kind, :, k, 0], sg.at[kind, k, 0], rg.at[kind, k, 0], gpeer(k, False))
            for k in (1, 2, 3)
        ]
        cs.append(
            remote(gkv.at[kind, :, 0, 0], gkv.at[kind, :, 0, 1], sg.at[kind, 0, 1], rg.at[kind, 0, 1], gpeer(0, True))
        )
        return cs

    c_k.wait()
    gkv[0, 0, 0, 0, 0] = rotate(
        kraw[...].astype(f32), cosb[pl.ds(piece, 32), :], sinb[pl.ds(piece, 32), :],
        lax.broadcasted_iota(i32, (32, 128), 1),
    ).astype(bf16)
    c_v.wait()
    for c in blk_c:
        c.start()
    spread_piece(0, 0)
    c_q.wait()
    qbuf[0] = rotate(qraw[...].astype(f32), cosb[...], sinb[...], lane256).astype(bf16)
    qx[0, 0:16, :] = qbuf[0, 0:16, :]
    qx[0, 16:32, :] = qbuf[0, 240:256, :]
    qx_c = [remote(qx.at[0], qx.at[k], ss.at[2, k], rs.at[2, k], xpeer(k)) for k in order]
    for c in qx_c + q_c:
        c.start()

    mine = x % 2

    def block_copy(kc, ko):
        mm = ((chip + kc) % 4) * 2 + ((1 - core) if ko else core)
        src, dst = wst.at[mm], wbuf.at[kc, ko]
        if kc:
            src, dst = src.at[mine], dst.at[mine]
        return remote(src, dst, sw.at[kc, ko], rw.at[kc, ko], gpeer(kc, ko == 1))

    big = req_s[128]
    first = jnp.int32(0)
    span = jnp.int32(0)
    run = jnp.int32(0)
    low8 = jnp.zeros((8, 128), i32)
    high8 = jnp.zeros((8, 128), i32)
    for r in range(REQS):
        size = len_s[r]
        hit = big == r
        first = jnp.where(hit, run, first)
        span = jnp.where(hit, size, span)
        low8 = jnp.where(lane8 == r, run, low8)
        run = run + size
        high8 = jnp.where(lane8 == r, run, high8)
    high8 = jnp.where(lane8 == big, low8, high8)

    def request_of(row):
        return jnp.where(row < big, row, jnp.where(row < big + BIG, big, row - (BIG - 1)))

    c_w.wait()
    for h in range(32):
        for n in range(4):
            wst[h % 8, n // 2, n % 2, (h // 8 + 4 - g) % 4] = wfull[n * 32 : n * 32 + 32, h * 128 : (h + 1) * 128]

    row128 = lax.broadcasted_iota(i32, (128, 128), 0)
    lane128 = lax.broadcasted_iota(i32, (128, 128), 1)
    key_z = (zh + 4 - (row128 >> 5)) & 3

    def mask_step(n, carry):
        rows = pl.ds(pl.multiple_of(128 * n, 128), 128)
        member = ((chip + 4 - n // 2) % 4) * 2 + (core + n) % 2
        inner = 32 * member + (row128 & 31)
        block_req = request_of(1024 * x + 256 * key_z + inner)
        bias[0, rows, :] = jnp.where(lane128 == block_req, 0.0, MASKED).astype(bf16)
        slot = 1024 * key_z + 256 * x + inner
        inside = ((slot - first) & 4095) < span
        bias[1, rows, :] = jnp.where(inside & (lane128 == big), 0.0, MASKED).astype(bf16)
        token = 1024 * seq + 128 * n + row128
        seen = (token >= low8[0:1, :]) & (token < high8[0:1, :])
        bias[2, rows, :] = jnp.where(seen, 0.0, MASKED).astype(bf16)
        return carry

    lax.fori_loop(0, 8, mask_step, 0)
    row256 = lax.broadcasted_iota(i32, (256, 128), 0)

    def hot_step(k, carry):
        row = 256 * (4 * ((x + 4 - k) % 4) + zh) + row256
        qhot[k] = jnp.where(lane256 == request_of(row), 1.0, 0.0).astype(bf16)
        return carry

    lax.fori_loop(0, 4, hot_step, 0)

    for c in cand_c:
        c.wait_recv()
    c_ck.wait()
    c_cv.wait()
    row32 = lax.broadcasted_iota(i32, (32, 128), 0)
    for t in (0, 1):
        chosen = jnp.zeros((32, 128), f32)
        for k in range(4):
            token = 4096 * ((x + 4 - k) % 4) + 1024 * zh + 256 * x + 32 * m + row32
            ok = (token >= first) & (token < first + span)
            chosen = jnp.where(ok, cand[t, k].astype(f32), chosen)
        gkv[1, t, 0, 0, 0] = chosen.astype(bf16)
    zc_c = [
        remote(gkv.at[1, :, 0, 0, 0], gkv.at[1, :, 0, 0, k], sz.at[1, k], rz.at[1, k], zpeer(k))
        for k in order
    ]
    for c in zc_c:
        c.start()
    spread_piece(1, 0)

    for c in qx_c:
        c.wait_recv()
    at0, at3 = x, (x + 1) % 4
    qs[0, 0:16, :] = qx[at0, 0:16, :]
    qs[0, 16:32, :] = qx[at3, 16:32, :]
    qs_c = [remote(qs.at[0], qs.at[k], ss.at[0, k], rs.at[0, k], zpeer(k)) for k in order]
    for c in qs_c:
        c.start()
    blk_c[1].wait_recv()
    spread_piece(0, 1)
    blk_c[2].wait_recv()
    spread_piece(0, 3)

    late = (row128 >> 4) & 1
    qs_row = 256 * key_z + (row128 & 15) + late * (3072 + 240)
    qs_hot = jnp.where(lane128 == request_of(qs_row), 1.0, 0.0).astype(bf16)
    zc_c[1].wait_recv()
    spread_piece(1, 1)
    zc_c[2].wait_recv()
    spread_piece(1, 3)
    blk_c[0].wait_recv()
    spread_piece(0, 2)
    zc_c[0].wait_recv()
    spread_piece(1, 2)
    blk_g, cache_g = spread_all(0), spread_all(1)
    w_c = [block_copy(kc, ko) for kc, ko in ((0, 1), (1, 0), (3, 0), (3, 1), (1, 1), (2, 0), (2, 1))]
    for c in w_c:
        c.start()

    def relay(kind, cs):
        fs = []
        for k in (1, 2, 3):
            cs[k - 1].wait_recv()
            f = remote(
                gkv.at[kind, :, k, 0], gkv.at[kind, :, k, 1], sg.at[kind, k, 1], rg.at[kind, k, 1], gpeer(0, True)
            )
            f.start()
            fs.append(f)
        return fs

    def relay_wait(cs, fs):
        cs[3].wait_recv()
        for f in fs:
            f.wait_recv()

    def attend(kind, k, v_t):
        k_aug = jnp.concatenate([gkv[kind, 0].reshape(1024, 128), bias[kind]], axis=1)
        q_aug = jnp.concatenate([qbuf[k], qhot[k]], axis=1)
        s = lax.dot_general(k_aug, q_aug, (((1,), (1,)), ((), ())), preferred_element_type=f32)
        top = jnp.max(s, axis=0, keepdims=True) * SCALE
        p = jnp.exp(s * SCALE - top)
        o = jnp.dot(v_t, p.astype(bf16), preferred_element_type=f32)
        return o[0:128, :], top, o[128:129, :]

    def values(kind):
        v = jnp.transpose(gkv[kind, 1].reshape(1024, 128))
        return jnp.concatenate([v, jnp.ones((16, 1024), bf16)], axis=0)

    def merge(o1, t1, l1, o2, t2, l2):
        top = jnp.maximum(t1, t2)
        w1, w2 = jnp.exp(t1 - top), jnp.exp(t2 - top)
        return o1 * w1 + o2 * w2, top, l1 * w1 + l2 * w2

    for c in qs_c:
        c.wait_recv()
    c_sk.wait()
    c_sv.wait()
    s = lax.dot_general(
        jnp.concatenate([qs[...].reshape(128, 128), qs_hot], axis=1),
        jnp.concatenate([cks[...], bias[2]], axis=1),
        (((1,), (1,)), ((), ())), preferred_element_type=f32,
    )
    top = jnp.max(s, axis=1, keepdims=True) * SCALE
    p = jnp.exp(s * SCALE - top)
    total = jnp.sum(p, axis=1, keepdims=True)
    o = jnp.dot(p.astype(bf16), cvs[...], preferred_element_type=f32) / total
    lse = jnp.broadcast_to(top + jnp.log(total), (128, 128))
    sp[:, 0] = o.reshape(4, 32, 128)
    sp[:, 1] = lse.reshape(4, 32, 128)
    sp_c = [
        remote(sp.at[k], spr.at[k], ss.at[1, k], rs.at[1, k], (x * 4 + (zh + 4 - k) % 4, head)) for k in order
    ]
    for c in sp_c:
        c.start()

    blk_f = relay(0, blk_g)
    for c in q_c:
        c.wait_recv()
    relay_wait(blk_g, blk_f)

    vt0 = values(0)

    def block_step(k, carry):
        o, t, l = attend(0, k, vt0)
        ob[k] = o
        tb[k] = jnp.broadcast_to(t, (8, 256))
        lb[k] = jnp.broadcast_to(l, (8, 256))
        return carry

    lax.fori_loop(0, 4, block_step, 0)

    cache_f = relay(1, cache_g)

    for c in sp_c:
        c.wait_recv()
    o, t, l = sp[0, 0], sp[0, 1], jnp.ones((32, 128), f32)
    for k in (1, 2, 3):
        o, t, l = merge(o, t, l, spr[k, 0], spr[k, 1], 1.0)
    pad = jnp.zeros((96, 128), f32)
    o, t, l = [jnp.transpose(jnp.concatenate([a, pad], axis=0)) for a in (o, t, l)]
    for at, half, shift, put in ((at0, 0, 0, lane128 < 16), (at3, 1, 96, lane128 >= 112)):
        cols = slice(128 * half, 128 * half + 128)
        o2, t2, l2 = [pltpu.roll(a, shift, 1) if shift else a for a in (o, t, l)]
        t2 = jnp.where(put, t2, MASKED)[0:8, :]
        l2 = l2[0:8, :]
        t1, l1 = tb[at, :, cols], lb[at, :, cols]
        top = jnp.maximum(t1, t2)
        w1, w2 = jnp.exp(t1 - top), jnp.exp(t2 - top)
        tb[at, :, cols] = top
        lb[at, :, cols] = l1 * w1 + l2 * w2
        ob[at, :, cols] = ob[at, :, cols] * w1[0:1, :] + jnp.where(put, o2, 0.0) * w2[0:1, :]

    relay_wait(cache_g, cache_f)
    vt1 = values(1)

    def back(k):
        return (((x + 4 - k) % 4) * 4 + zh, head)

    def o_copy(k):
        return remote(osend.at[k], orecv.at[k], so.at[k], ro.at[k], back(k))

    def l_copy(k):
        return remote(ssend.at[k], srecv.at[k], sl.at[k], rl.at[k], back(k))

    def cache_step(n, carry):
        k = (2 + 3 * n + 3 * (n // 2) + 2 * (n // 3)) % 4
        o, t, l = attend(1, k, vt1)
        o, t, l = merge(ob[k], tb[k, 0:1, :], lb[k, 0:1, :], o, t, l)
        osend[k] = (o * (1.0 / l)).astype(bf16)
        ssend[k] = jnp.broadcast_to(t + jnp.log(l), (8, 256))

        @pl.when(n < 3)
        def _():
            o_copy(k).start()
            l_copy(k).start()

        return carry

    lax.fori_loop(0, 4, cache_step, 0)
    o_c = [f(k) for k in order for f in (o_copy, l_copy)]

    for c in w_c[1:]:
        c.wait_recv()
    w_x = [
        remote(wbuf.at[1:4, :, mine, n], wbuf.at[1:4, :, mine, n], sx.at[n], rx.at[n], xpeer(k))
        for n, k in ((0, 3), (1, 1))
    ]
    for c in w_x:
        c.start()
    for c in cand_c + q_c + blk_c + zc_c + blk_g + blk_f + cache_g + cache_f + qx_c + qs_c + sp_c:
        c.wait_send()
    for c in o_c:
        c.wait_recv()

    lses = [ssend[0, 0:1, :]] + [srecv[k, 0:1, :] for k in (1, 2, 3)]
    top = jnp.maximum(jnp.maximum(lses[0], lses[1]), jnp.maximum(lses[2], lses[3]))
    weights = [jnp.exp(l - top) for l in lses]
    total = 1.0 / (weights[0] + weights[1] + weights[2] + weights[3])

    def h_copies(half):
        cs = [
            remote(
                hbuf.at[half, 0, 0], hbuf.at[half, k, 0], sh.at[half, k, 0], rh.at[half, k, 0], gpeer(k, False)
            )
            for k in order
        ]
        cs.append(
            remote(hbuf.at[half, 0, 0], hbuf.at[half, 0, 1], sh.at[half, 0, 1], rh.at[half, 0, 1], gpeer(0, True))
        )
        return cs

    for k in range(4):
        wts[k] = jnp.broadcast_to(weights[k] * total, (8, 256))

    def heads_step(half, carry):
        cols = pl.ds(pl.multiple_of(128 * half, 128), 128)
        heads = osend[0, :, cols].astype(f32) * wts[0, 0:1, cols]
        for k in (1, 2, 3):
            heads = heads + orecv[k, :, cols].astype(f32) * wts[k, 0:1, cols]
        hbuf[half, 0, 0] = jnp.transpose(heads).astype(bf16)
        for c in h_copies(half):
            c.start()
        return carry

    lax.fori_loop(0, 2, heads_step, 0)
    h_c = [h_copies(0), h_copies(1)]
    h_f = []
    for half in (0, 1):
        fs = []
        for n, k in enumerate(order):
            h_c[half][n].wait_recv()
            f = remote(
                hbuf.at[half, k, 0], hbuf.at[half, k, 1], sh.at[half, k, 1], rh.at[half, k, 1], gpeer(0, True)
            )
            f.start()
            fs.append(f)
        h_f.append(fs)

    for c in w_c[:1] + w_x:
        c.wait_recv()
    wbuf[0, 0] = wst[m]

    def mid_copy(half):
        return remote(psend.at[half, 2], precv.at[half], sf.at[half, 0], rf.at[half, 0], fpeer(1 + 2 * half))

    def final_copy(half, j):
        rows = pl.ds(pl.multiple_of(128 * half, 128), 128)
        return remote(psend.at[half, j], near_ref.at[j // 2, rows], sf.at[half, j], rf.at[half, j], fpeer(j))

    def mine_copy(half):
        rows = pl.ds(pl.multiple_of(128 * half, 128), 128)
        return pltpu.make_async_copy(own.at[half, 0], mine_ref.at[rows], loc.at[half])

    def project_step(half, carry):
        for c in h_copies(half)[3:]:
            c.wait_recv()
        for k in order:
            remote(
                hbuf.at[half, k, 0], hbuf.at[half, k, 1], sh.at[half, k, 1], rh.at[half, k, 1], gpeer(0, True)
            ).wait_recv()
        lhs = jnp.concatenate([hbuf[half, kc, ko] for kc in range(4) for ko in (0, 1)], axis=1)
        rhs = jnp.concatenate([wbuf[:, :, :, :, j].reshape(1024, 128) for j in range(4)], axis=1)
        acc = jnp.dot(lhs, rhs, preferred_element_type=f32)
        for j in range(4):
            own[half, j] = acc[:, j * 128 : (j + 1) * 128]
            psend[half, j] = own[half, j].astype(bf16)
        mid_copy(half).start()
        final_copy(half, 3 - 2 * half).start()
        mine_copy(half).start()
        return carry

    lax.fori_loop(0, 2, project_step, 0)
    mids = [mid_copy(0), mid_copy(1)]
    finals = [final_copy(0, 3), final_copy(1, 1)]
    for c in o_c + h_c[0] + h_c[1] + h_f[0] + h_f[1]:
        c.wait_send()
    for half in (0, 1):
        fwd = 1 if half == 0 else 3
        mids[half].wait_recv()
        psend[half, fwd] = (own[half, fwd] + precv[half].astype(f32)).astype(bf16)
        far = final_copy(half, fwd)
        far.start()
        finals.append(far)
    for c in w_c + w_x:
        c.wait_send()
    for half in (0, 1):
        finals[half].wait_recv()
        finals[2 + half].wait_recv()
        mine_copy(half).wait()

    sent = mids + finals
    for c in sent:
        c.wait_send()


def shards(queries, block_keys, block_values, cache_keys, cache_values, lengths, row_request, positions, out_weight):
    dma = pltpu.SemaphoreType.DMA
    vmem = pltpu.VMEM
    mine, near = pl.pallas_call(
        kernel,
        out_shape=(jax.ShapeDtypeStruct((256, HD), f32), jax.ShapeDtypeStruct((2, 256, HD), bf16)),
        in_specs=[pl.BlockSpec(memory_space=pl.ANY)] * 10,
        out_specs=(pl.BlockSpec(memory_space=pl.ANY), pl.BlockSpec(memory_space=pl.ANY)),
        scratch_shapes=[
            pltpu.SMEM((8,), i32),
            pltpu.SMEM((256,), i32),
            vmem((2, 128), i32),
            vmem((2, 128), i32),
            vmem((256, 128), bf16),
            vmem((32, 128), bf16),
            vmem((256, 128), f32),
            vmem((256, 128), f32),
            vmem((4, 256, 128), bf16),
            vmem((4, 256, 128), bf16),
            vmem((2, 4, 32, 128), bf16),
            vmem((2, 2, 4, 2, 4, 32, 128), bf16),
            vmem((3, 1024, 128), bf16),
            vmem((1024, 128), bf16),
            vmem((1024, 128), bf16),
            vmem((4, 32, 128), bf16),
            vmem((4, 32, 128), bf16),
            vmem((4, 2, 32, 128), f32),
            vmem((4, 2, 32, 128), f32),
            vmem((4, 128, 256), f32),
            vmem((4, 8, 256), f32),
            vmem((4, 8, 256), f32),
            vmem((4, 128, 256), bf16),
            vmem((4, 8, 256), f32),
            vmem((4, 128, 256), bf16),
            vmem((4, 8, 256), f32),
            vmem((2, 4, 2, 128, 128), bf16),
            vmem((128, 4096), bf16),
            vmem((8, 2, 2, 4, 32, 128), bf16),
            vmem((4, 2, 2, 2, 4, 32, 128), bf16),
            vmem((2, 4, 128, 128), bf16),
            vmem((2, 128, 128), bf16),
            vmem((2, 4, 128, 128), f32),
            vmem((4, 8, 256), f32),
            dma((12,)),
            dma((4,)), dma((4,)),
            dma((2, 4)), dma((2, 4)),
            dma((2, 4)), dma((2, 4)),
            dma((2, 4, 2)), dma((2, 4, 2)),
            dma((3, 4)), dma((3, 4)),
            dma((4, 2)), dma((4, 2)),
            dma((2,)), dma((2,)),
            dma((4,)), dma((4,)),
            dma((4,)), dma((4,)),
            dma((2, 4, 2)), dma((2, 4, 2)),
            dma((2, 4)), dma((2, 4)),
        ],
        compiler_params=pltpu.CompilerParams(
            collective_id=0, has_side_effects=True, vmem_limit_bytes=63 * 1024 * 1024
        ),
    )(
        lengths, row_request, row_request.reshape(2, 128), positions.reshape(2, 128),
        queries, block_keys, block_values, cache_keys, cache_values, out_weight,
    )
    return (mine + near[0].astype(f32) + near[1].astype(f32)).astype(bf16)


def solution(mesh):
    placed = (
        P("seq", "head"),
        P("seq", None),
        P("seq", None),
        P(None, "seq", None),
        P(None, "seq", None),
        P(),
        P("seq"),
        P("seq"),
        P("head", None),
    )
    return jax.shard_map(
        shards, mesh=mesh, in_specs=placed, out_specs=P("seq", "head"), check_vma=False
    )
```

```python
import math

import jax
import jax.numpy as jnp
from jax import lax
from jax.experimental import pallas as pl
from jax.experimental.pallas import tpu as pltpu
from jax.sharding import PartitionSpec as P

HD = 128
REQS = 8
BIG = 4089
MASKED = -1e30
SCALE = 1.0 / math.sqrt(HD)

bf16 = jnp.bfloat16
f32 = jnp.float32
i32 = jnp.int32
MESH = pl.DeviceIdType.MESH


def kernel(
    len_h, req_h, rows_h, pos_h, q_h, bk_h, bv_h, ck_h, cv_h, w_h,
    mine_ref, near_ref,
    len_s, req_s, req_v, pos_v, qraw, kraw, cosb, sinb, qbuf, qhot, cand, gkv, bias, cks, cvs, qx, qs, sp, spr,
    ob, tb, lb, osend, ssend, orecv, srecv, hbuf, wfull, wst, wbuf, psend, precv, own, wts,
    loc, sq, rq, sc, rc, sz, rz, sg, rg, sd, rd, ss, rs, sw, rw, sx, rx, so, ro, sl, rl, sh, rh, sf, rf,
):
    seq = lax.axis_index("seq")
    head = lax.axis_index("head")
    x, zh = seq // 4, seq % 4
    g, m = head // 8, head % 8
    chip, core = m // 2, m % 2

    def xpeer(k):
        return (((x + k) % 4) * 4 + zh, head)

    def zpeer(k):
        return (x * 4 + (zh + k) % 4, head)

    def gpeer(k, other):
        c = (1 - core) if other else core
        return (seq, g * 8 + ((chip + k) % 4) * 2 + c)

    def fpeer(k):
        return (seq, ((g + k) % 4) * 8 + m)

    def remote(src, dst, ssem, rsem, peer):
        return pltpu.make_async_remote_copy(
            src_ref=src, dst_ref=dst, send_sem=ssem, recv_sem=rsem,
            device_id=peer, device_id_type=MESH,
        )

    piece = pl.multiple_of(32 * m, 32)
    gcol = pl.multiple_of(g * 128, 128)
    mycand = pl.multiple_of(256 * x + 32 * m, 32)
    c_q = pltpu.make_async_copy(q_h, qraw, loc.at[0])
    c_k = pltpu.make_async_copy(bk_h.at[pl.ds(piece, 32), pl.ds(gcol, 128)], kraw, loc.at[1])
    c_v = pltpu.make_async_copy(
        bv_h.at[pl.ds(piece, 32), pl.ds(gcol, 128)], gkv.at[0, 1, 0, 0, 0], loc.at[2]
    )
    c_ck = pltpu.make_async_copy(ck_h.at[g, pl.ds(mycand, 32)], cand.at[0, 0], loc.at[3])
    c_cv = pltpu.make_async_copy(cv_h.at[g, pl.ds(mycand, 32)], cand.at[1, 0], loc.at[4])
    c_sk = pltpu.make_async_copy(ck_h.at[g], cks, loc.at[5])
    c_sv = pltpu.make_async_copy(cv_h.at[g], cvs, loc.at[6])
    c_small = [
        pltpu.make_async_copy(src, dst, loc.at[8 + n])
        for n, (src, dst) in enumerate(((rows_h, req_v), (pos_h, pos_v), (len_h, len_s), (req_h, req_s)))
    ]
    c_w = pltpu.make_async_copy(w_h, wfull, loc.at[7])
    for c in c_small + [c_k, c_v, c_q, c_ck, c_cv, c_sk, c_sv, c_w]:
        c.start()

    barrier = pltpu.get_barrier_semaphore()
    peers = [xpeer(k) for k in (1, 2, 3)] + [zpeer(k) for k in (1, 2, 3)]
    peers += [gpeer(k, o) for k in range(4) for o in (False, True) if k or o]
    peers += [fpeer(k) for k in (1, 3)]
    for peer in peers:
        pl.semaphore_signal(barrier, inc=1, device_id=peer, device_id_type=MESH)

    pl.semaphore_wait(barrier, len(peers))

    order = (2, 1, 3)
    place = (0, 1, 3, 2)
    cand_c, q_c, blk_c = [], [], []
    for k in order:
        start = pl.multiple_of(256 * ((x + k) % 4) + 32 * m, 32)
        cand_c.append(remote(ck_h.at[g, pl.ds(start, 32)], cand.at[0, k], sc.at[0, k], rc.at[0, k], xpeer(k)))
        cand_c.append(remote(cv_h.at[g, pl.ds(start, 32)], cand.at[1, k], sc.at[1, k], rc.at[1, k], xpeer(k)))
        blk_c.append(
            remote(gkv.at[0, :, 0, 0, 0], gkv.at[0, :, 0, 0, place[k]], sz.at[0, k], rz.at[0, k], zpeer(k))
        )
        q_c.append(remote(qbuf.at[0], qbuf.at[k], sq.at[k], rq.at[k], xpeer(k)))
    for c in cand_c:
        c.start()

    for c in c_small:
        c.wait()
    row_len = jnp.zeros((2, 128), i32)
    for r in range(REQS):
        row_len = jnp.where(req_v[...] == r, len_s[r], row_len)
    rotary = (row_len + pos_v[...]).astype(f32)
    spread = jnp.concatenate(
        [jnp.transpose(jnp.broadcast_to(rotary[h : h + 1, :], (128, 128))) for h in (0, 1)], axis=0
    )
    lane8 = lax.broadcasted_iota(i32, (8, 128), 1)
    turns = jnp.zeros((8, 128), f32)
    for k in range(HD // 4):
        turns = jnp.where(
            (lane8 < 64) & (lane8 % 32 == k), 10000.0 ** (-k / (HD // 4)) / (2.0 * math.pi), turns
        )
    lane256 = lax.broadcasted_iota(i32, (256, 128), 1)
    angle = spread * turns[0:1, :]
    angle = (angle - jnp.floor(angle + 0.5)) * (2.0 * math.pi)
    square = angle * angle
    cosine = jnp.full((256, 128), 1.0 / math.factorial(16), f32)
    sine = jnp.full((256, 128), -1.0 / math.factorial(15), f32)
    for n in range(7, -1, -1):
        cosine = cosine * square + (-1.0) ** n / math.factorial(2 * n)
    for n in range(6, -1, -1):
        sine = sine * square + (-1.0) ** n / math.factorial(2 * n + 1)
    sine = sine * angle
    cosb[...] = cosine
    sinb[...] = jnp.where(lane256 < 32, -sine, sine)

    def rotate(v, cosine, signed, lane):
        partner = jnp.where(lane < 32, pltpu.roll(v, 96, 1), pltpu.roll(v, 32, 1))
        return v * cosine + partner * signed

    def spread_piece(kind, z):
        src = gkv.at[kind, :, 0, 0, place[z]]
        for k in (3, 1, 2):
            remote(
                src, gkv.at[kind, :, k, 0, place[z]], sg.at[kind, k, 0], rg.at[kind, k, 0], gpeer(k, False)
            ).start()
        remote(
            src, gkv.at[kind, :, 0, 1, place[z]], sg.at[kind, 0, 1], rg.at[kind, 0, 1], gpeer(0, True)
        ).start()

    def far_copies():
        return [
            remote(gkv.at[1, :, 0, 0, 3], gkv.at[1, :, k, o, 3], sd.at[k, o], rd.at[k, o], gpeer(k, o == 1))
            for k in (3, 1, 2, 0) for o in (0, 1) if k or o
        ]

    def spread_all(kind):
        upto = slice(0, 4 - kind)
        src = gkv.at[kind, :, 0, 0, upto]
        cs = [
            remote(src, gkv.at[kind, :, k, 0, upto], sg.at[kind, k, 0], rg.at[kind, k, 0], gpeer(k, False))
            for k in (1, 2, 3)
        ]
        cs.append(remote(src, gkv.at[kind, :, 0, 1, upto], sg.at[kind, 0, 1], rg.at[kind, 0, 1], gpeer(0, True)))
        return cs

    c_k.wait()
    gkv[0, 0, 0, 0, 0] = rotate(
        kraw[...].astype(f32), cosb[pl.ds(piece, 32), :], sinb[pl.ds(piece, 32), :],
        lax.broadcasted_iota(i32, (32, 128), 1),
    ).astype(bf16)
    c_v.wait()
    for c in blk_c:
        c.start()
    spread_piece(0, 0)
    c_q.wait()
    qbuf[0] = rotate(qraw[...].astype(f32), cosb[...], sinb[...], lane256).astype(bf16)
    qx[0, 0:16, :] = qbuf[0, 0:16, :]
    qx[0, 16:32, :] = qbuf[0, 240:256, :]
    qx_c = [remote(qx.at[0], qx.at[k], ss.at[2, k], rs.at[2, k], xpeer(k)) for k in order]
    for c in qx_c + q_c:
        c.start()

    mine = x % 2

    def block_copy(kc, ko):
        mm = ((chip + kc) % 4) * 2 + ((1 - core) if ko else core)
        src, dst = wst.at[mm], wbuf.at[kc, ko]
        if kc:
            src, dst = src.at[mine], dst.at[mine]
        return remote(src, dst, sw.at[kc, ko], rw.at[kc, ko], gpeer(kc, ko == 1))

    big = req_s[128]
    first = jnp.int32(0)
    span = jnp.int32(0)
    run = jnp.int32(0)
    low8 = jnp.zeros((8, 128), i32)
    high8 = jnp.zeros((8, 128), i32)
    for r in range(REQS):
        size = len_s[r]
        hit = big == r
        first = jnp.where(hit, run, first)
        span = jnp.where(hit, size, span)
        low8 = jnp.where(lane8 == r, run, low8)
        run = run + size
        high8 = jnp.where(lane8 == r, run, high8)
    high8 = jnp.where(lane8 == big, low8, high8)

    def request_of(row):
        return jnp.where(row < big, row, jnp.where(row < big + BIG, big, row - (BIG - 1)))

    c_w.wait()
    for h in range(32):
        for n in range(4):
            wst[h % 8, n // 2, n % 2, (h // 8 + 4 - g) % 4] = wfull[n * 32 : n * 32 + 32, h * 128 : (h + 1) * 128]

    row128 = lax.broadcasted_iota(i32, (128, 128), 0)
    lane128 = lax.broadcasted_iota(i32, (128, 128), 1)
    from_z = (zh + 4 - (row128 >> 5)) & 3
    lies = (row128 >> 5) & 3
    key_z = (zh + 4 - (lies ^ (lies >> 1))) & 3

    def mask_step(n, carry):
        rows = pl.ds(pl.multiple_of(128 * n, 128), 128)
        member = ((chip + 4 - n // 2) % 4) * 2 + (core + n) % 2
        inner = 32 * member + (row128 & 31)
        block_req = request_of(1024 * x + 256 * key_z + inner)
        bias[0, rows, :] = jnp.where(lane128 == block_req, 0.0, MASKED).astype(bf16)
        slot = 1024 * key_z + 256 * x + inner
        inside = ((slot - first) & 4095) < span
        bias[1, rows, :] = jnp.where(inside & (lane128 == big), 0.0, MASKED).astype(bf16)
        token = 1024 * seq + 128 * n + row128
        seen = (token >= low8[0:1, :]) & (token < high8[0:1, :])
        bias[2, rows, :] = jnp.where(seen, 0.0, MASKED).astype(bf16)
        return carry

    lax.fori_loop(0, 8, mask_step, 0)
    row256 = lax.broadcasted_iota(i32, (256, 128), 0)

    def hot_step(k, carry):
        row = 256 * (4 * ((x + 4 - k) % 4) + zh) + row256
        qhot[k] = jnp.where(lane256 == request_of(row), 1.0, 0.0).astype(bf16)
        return carry

    lax.fori_loop(0, 4, hot_step, 0)

    for c in cand_c:
        c.wait_recv()
    c_ck.wait()
    c_cv.wait()
    row32 = lax.broadcasted_iota(i32, (32, 128), 0)
    for t in (0, 1):
        chosen = jnp.zeros((32, 128), f32)
        for k in range(4):
            token = 4096 * ((x + 4 - k) % 4) + 1024 * zh + 256 * x + 32 * m + row32
            ok = (token >= first) & (token < first + span)
            chosen = jnp.where(ok, cand[t, k].astype(f32), chosen)
        gkv[1, t, 0, 0, 0] = chosen.astype(bf16)
    zc_c = [
        remote(gkv.at[1, :, 0, 0, 0], gkv.at[1, :, 0, 0, place[k]], sz.at[1, k], rz.at[1, k], zpeer(k))
        for k in order
    ]
    for c in zc_c:
        c.start()
    spread_piece(1, 0)

    for c in qx_c:
        c.wait_recv()
    at0, at3 = x, (x + 1) % 4
    qs[0, 0:16, :] = qx[at0, 0:16, :]
    qs[0, 16:32, :] = qx[at3, 16:32, :]
    qs_c = [remote(qs.at[0], qs.at[k], ss.at[0, k], rs.at[0, k], zpeer(k)) for k in order]
    for c in qs_c:
        c.start()
    blk_c[1].wait_recv()
    spread_piece(0, 1)
    blk_c[2].wait_recv()
    spread_piece(0, 3)

    late = (row128 >> 4) & 1
    qs_row = 256 * from_z + (row128 & 15) + late * (3072 + 240)
    qs_hot = jnp.where(lane128 == request_of(qs_row), 1.0, 0.0).astype(bf16)
    zc_c[1].wait_recv()
    spread_piece(1, 1)
    zc_c[2].wait_recv()
    spread_piece(1, 3)
    blk_c[0].wait_recv()
    spread_piece(0, 2)
    zc_c[0].wait_recv()
    far_c = far_copies()
    for c in far_c:
        c.start()
    blk_g, cache_g = spread_all(0), spread_all(1)
    w_c = [block_copy(kc, ko) for kc, ko in ((0, 1), (1, 0), (3, 0), (3, 1), (1, 1), (2, 0), (2, 1))]
    for c in w_c:
        c.start()

    def relay(kind, cs):
        upto = slice(0, 4 - kind)
        fs = []
        for k in (1, 2, 3):
            cs[k - 1].wait_recv()
            f = remote(
                gkv.at[kind, :, k, 0, upto], gkv.at[kind, :, k, 1, upto], sg.at[kind, k, 1], rg.at[kind, k, 1],
                gpeer(0, True),
            )
            f.start()
            fs.append(f)
        return fs

    def relay_wait(cs, fs):
        cs[3].wait_recv()
        for f in fs:
            f.wait_recv()

    def attend(kind, k, v_t):
        k_aug = jnp.concatenate([gkv[kind, 0].reshape(1024, 128), bias[kind]], axis=1)
        q_aug = jnp.concatenate([qbuf[k], qhot[k]], axis=1)
        s = lax.dot_general(k_aug, q_aug, (((1,), (1,)), ((), ())), preferred_element_type=f32)
        top = jnp.max(s, axis=0, keepdims=True) * SCALE
        p = jnp.exp(s * SCALE - top)
        o = jnp.dot(v_t, p.astype(bf16), preferred_element_type=f32)
        return o[0:128, :], top, o[128:129, :]

    def values(kind):
        v = jnp.transpose(gkv[kind, 1].reshape(1024, 128))
        return jnp.concatenate([v, jnp.ones((16, 1024), bf16)], axis=0)

    def merge(o1, t1, l1, o2, t2, l2):
        top = jnp.maximum(t1, t2)
        w1, w2 = jnp.exp(t1 - top), jnp.exp(t2 - top)
        return o1 * w1 + o2 * w2, top, l1 * w1 + l2 * w2

    for c in qs_c:
        c.wait_recv()
    c_sk.wait()
    c_sv.wait()
    s = lax.dot_general(
        jnp.concatenate([qs[...].reshape(128, 128), qs_hot], axis=1),
        jnp.concatenate([cks[...], bias[2]], axis=1),
        (((1,), (1,)), ((), ())), preferred_element_type=f32,
    )
    top = jnp.max(s, axis=1, keepdims=True) * SCALE
    p = jnp.exp(s * SCALE - top)
    total = jnp.sum(p, axis=1, keepdims=True)
    o = jnp.dot(p.astype(bf16), cvs[...], preferred_element_type=f32) / total
    lse = jnp.broadcast_to(top + jnp.log(total), (128, 128))
    sp[:, 0] = o.reshape(4, 32, 128)
    sp[:, 1] = lse.reshape(4, 32, 128)
    sp_c = [
        remote(sp.at[k], spr.at[k], ss.at[1, k], rs.at[1, k], (x * 4 + (zh + 4 - k) % 4, head)) for k in order
    ]
    for c in sp_c:
        c.start()

    blk_f = relay(0, blk_g)
    for c in q_c:
        c.wait_recv()
    cache_f = relay(1, cache_g)
    relay_wait(blk_g, blk_f)

    vt0 = values(0)

    def block_step(k, carry):
        o, t, l = attend(0, k, vt0)
        ob[k] = o
        tb[k] = jnp.broadcast_to(t, (8, 256))
        lb[k] = jnp.broadcast_to(l, (8, 256))
        return carry

    lax.fori_loop(0, 4, block_step, 0)


    for c in sp_c:
        c.wait_recv()
    o, t, l = sp[0, 0], sp[0, 1], jnp.ones((32, 128), f32)
    for k in (1, 2, 3):
        o, t, l = merge(o, t, l, spr[k, 0], spr[k, 1], 1.0)
    pad = jnp.zeros((96, 128), f32)
    o, t, l = [jnp.transpose(jnp.concatenate([a, pad], axis=0)) for a in (o, t, l)]
    for at, half, shift, put in ((at0, 0, 0, lane128 < 16), (at3, 1, 96, lane128 >= 112)):
        cols = slice(128 * half, 128 * half + 128)
        o2, t2, l2 = [pltpu.roll(a, shift, 1) if shift else a for a in (o, t, l)]
        t2 = jnp.where(put, t2, MASKED)[0:8, :]
        l2 = l2[0:8, :]
        t1, l1 = tb[at, :, cols], lb[at, :, cols]
        top = jnp.maximum(t1, t2)
        w1, w2 = jnp.exp(t1 - top), jnp.exp(t2 - top)
        tb[at, :, cols] = top
        lb[at, :, cols] = l1 * w1 + l2 * w2
        ob[at, :, cols] = ob[at, :, cols] * w1[0:1, :] + jnp.where(put, o2, 0.0) * w2[0:1, :]

    relay_wait(cache_g, cache_f)
    for c in far_c:
        c.wait_recv()
    vt1 = values(1)

    def back(k):
        return (((x + 4 - k) % 4) * 4 + zh, head)

    def o_copy(k):
        return remote(osend.at[k], orecv.at[k], so.at[k], ro.at[k], back(k))

    def l_copy(k):
        return remote(ssend.at[k], srecv.at[k], sl.at[k], rl.at[k], back(k))

    def cache_step(n, carry):
        k = (2 + 3 * n + 3 * (n // 2) + 2 * (n // 3)) % 4
        o, t, l = attend(1, k, vt1)
        o, t, l = merge(ob[k], tb[k, 0:1, :], lb[k, 0:1, :], o, t, l)
        osend[k] = (o * (1.0 / l)).astype(bf16)
        ssend[k] = jnp.broadcast_to(t + jnp.log(l), (8, 256))

        @pl.when(n < 3)
        def _():
            o_copy(k).start()
            l_copy(k).start()

        return carry

    lax.fori_loop(0, 4, cache_step, 0)
    o_c = [f(k) for k in order for f in (o_copy, l_copy)]

    for c in w_c[1:]:
        c.wait_recv()
    w_x = [
        remote(wbuf.at[1:4, :, mine, n], wbuf.at[1:4, :, mine, n], sx.at[n], rx.at[n], xpeer(k))
        for n, k in ((0, 3), (1, 1))
    ]
    for c in w_x:
        c.start()
    for c in cand_c + q_c + blk_c + zc_c + blk_g + blk_f + cache_g + cache_f + far_c + qx_c + qs_c + sp_c:
        c.wait_send()
    for c in o_c:
        c.wait_recv()

    lses = [ssend[0, 0:1, :]] + [srecv[k, 0:1, :] for k in (1, 2, 3)]
    top = jnp.maximum(jnp.maximum(lses[0], lses[1]), jnp.maximum(lses[2], lses[3]))
    weights = [jnp.exp(l - top) for l in lses]
    total = 1.0 / (weights[0] + weights[1] + weights[2] + weights[3])

    def h_copies(half):
        cs = [
            remote(
                hbuf.at[half, 0, 0], hbuf.at[half, k, 0], sh.at[half, k, 0], rh.at[half, k, 0], gpeer(k, False)
            )
            for k in order
        ]
        cs.append(
            remote(hbuf.at[half, 0, 0], hbuf.at[half, 0, 1], sh.at[half, 0, 1], rh.at[half, 0, 1], gpeer(0, True))
        )
        return cs

    for k in range(4):
        wts[k] = jnp.broadcast_to(weights[k] * total, (8, 256))

    def heads_step(half, carry):
        cols = pl.ds(pl.multiple_of(128 * half, 128), 128)
        heads = osend[0, :, cols].astype(f32) * wts[0, 0:1, cols]
        for k in (1, 2, 3):
            heads = heads + orecv[k, :, cols].astype(f32) * wts[k, 0:1, cols]
        hbuf[half, 0, 0] = jnp.transpose(heads).astype(bf16)
        for c in h_copies(half):
            c.start()
        return carry

    lax.fori_loop(0, 2, heads_step, 0)
    h_c = [h_copies(0), h_copies(1)]
    h_f = []
    for half in (0, 1):
        fs = []
        for n, k in enumerate(order):
            h_c[half][n].wait_recv()
            f = remote(
                hbuf.at[half, k, 0], hbuf.at[half, k, 1], sh.at[half, k, 1], rh.at[half, k, 1], gpeer(0, True)
            )
            f.start()
            fs.append(f)
        h_f.append(fs)

    for c in w_c[:1] + w_x:
        c.wait_recv()
    wbuf[0, 0] = wst[m]

    def mid_copy(half):
        return remote(psend.at[half, 2], precv.at[half], sf.at[half, 0], rf.at[half, 0], fpeer(1 + 2 * half))

    def final_copy(half, j):
        rows = pl.ds(pl.multiple_of(128 * half, 128), 128)
        return remote(psend.at[half, j], near_ref.at[j // 2, rows], sf.at[half, j], rf.at[half, j], fpeer(j))

    def mine_copy(half):
        rows = pl.ds(pl.multiple_of(128 * half, 128), 128)
        return pltpu.make_async_copy(own.at[half, 0], mine_ref.at[rows], loc.at[half])

    def project_step(half, carry):
        for c in h_copies(half)[3:]:
            c.wait_recv()
        for k in order:
            remote(
                hbuf.at[half, k, 0], hbuf.at[half, k, 1], sh.at[half, k, 1], rh.at[half, k, 1], gpeer(0, True)
            ).wait_recv()
        lhs = jnp.concatenate([hbuf[half, kc, ko] for kc in range(4) for ko in (0, 1)], axis=1)
        rhs = jnp.concatenate([wbuf[:, :, :, :, j].reshape(1024, 128) for j in range(4)], axis=1)
        acc = jnp.dot(lhs, rhs, preferred_element_type=f32)
        for j in range(4):
            own[half, j] = acc[:, j * 128 : (j + 1) * 128]
            psend[half, j] = own[half, j].astype(bf16)
        mid_copy(half).start()
        final_copy(half, 3 - 2 * half).start()
        mine_copy(half).start()
        return carry

    lax.fori_loop(0, 2, project_step, 0)
    mids = [mid_copy(0), mid_copy(1)]
    finals = [final_copy(0, 3), final_copy(1, 1)]
    for c in o_c + h_c[0] + h_c[1] + h_f[0] + h_f[1]:
        c.wait_send()
    for half in (0, 1):
        fwd = 1 if half == 0 else 3
        mids[half].wait_recv()
        psend[half, fwd] = (own[half, fwd] + precv[half].astype(f32)).astype(bf16)
        far = final_copy(half, fwd)
        far.start()
        finals.append(far)
    for c in w_c + w_x:
        c.wait_send()
    for half in (0, 1):
        finals[half].wait_recv()
        finals[2 + half].wait_recv()
        mine_copy(half).wait()

    sent = mids + finals
    for c in sent:
        c.wait_send()


def shards(queries, block_keys, block_values, cache_keys, cache_values, lengths, row_request, positions, out_weight):
    dma = pltpu.SemaphoreType.DMA
    vmem = pltpu.VMEM
    mine, near = pl.pallas_call(
        kernel,
        out_shape=(jax.ShapeDtypeStruct((256, HD), f32), jax.ShapeDtypeStruct((2, 256, HD), bf16)),
        in_specs=[pl.BlockSpec(memory_space=pl.ANY)] * 10,
        out_specs=(pl.BlockSpec(memory_space=pl.ANY), pl.BlockSpec(memory_space=pl.ANY)),
        scratch_shapes=[
            pltpu.SMEM((8,), i32),
            pltpu.SMEM((256,), i32),
            vmem((2, 128), i32),
            vmem((2, 128), i32),
            vmem((256, 128), bf16),
            vmem((32, 128), bf16),
            vmem((256, 128), f32),
            vmem((256, 128), f32),
            vmem((4, 256, 128), bf16),
            vmem((4, 256, 128), bf16),
            vmem((2, 4, 32, 128), bf16),
            vmem((2, 2, 4, 2, 4, 32, 128), bf16),
            vmem((3, 1024, 128), bf16),
            vmem((1024, 128), bf16),
            vmem((1024, 128), bf16),
            vmem((4, 32, 128), bf16),
            vmem((4, 32, 128), bf16),
            vmem((4, 2, 32, 128), f32),
            vmem((4, 2, 32, 128), f32),
            vmem((4, 128, 256), f32),
            vmem((4, 8, 256), f32),
            vmem((4, 8, 256), f32),
            vmem((4, 128, 256), bf16),
            vmem((4, 8, 256), f32),
            vmem((4, 128, 256), bf16),
            vmem((4, 8, 256), f32),
            vmem((2, 4, 2, 128, 128), bf16),
            vmem((128, 4096), bf16),
            vmem((8, 2, 2, 4, 32, 128), bf16),
            vmem((4, 2, 2, 2, 4, 32, 128), bf16),
            vmem((2, 4, 128, 128), bf16),
            vmem((2, 128, 128), bf16),
            vmem((2, 4, 128, 128), f32),
            vmem((4, 8, 256), f32),
            dma((12,)),
            dma((4,)), dma((4,)),
            dma((2, 4)), dma((2, 4)),
            dma((2, 4)), dma((2, 4)),
            dma((2, 4, 2)), dma((2, 4, 2)),
            dma((4, 2)), dma((4, 2)),
            dma((3, 4)), dma((3, 4)),
            dma((4, 2)), dma((4, 2)),
            dma((2,)), dma((2,)),
            dma((4,)), dma((4,)),
            dma((4,)), dma((4,)),
            dma((2, 4, 2)), dma((2, 4, 2)),
            dma((2, 4)), dma((2, 4)),
        ],
        compiler_params=pltpu.CompilerParams(
            collective_id=0, has_side_effects=True, vmem_limit_bytes=63 * 1024 * 1024
        ),
    )(
        lengths, row_request, row_request.reshape(2, 128), positions.reshape(2, 128),
        queries, block_keys, block_values, cache_keys, cache_values, out_weight,
    )
    return (mine + near[0].astype(f32) + near[1].astype(f32)).astype(bf16)


def solution(mesh):
    placed = (
        P("seq", "head"),
        P("seq", None),
        P("seq", None),
        P(None, "seq", None),
        P(None, "seq", None),
        P(),
        P("seq"),
        P("seq"),
        P("head", None),
    )
    return jax.shard_map(
        shards, mesh=mesh, in_specs=placed, out_specs=P("seq", "head"), check_vma=False
    )
```
